256 devices in a mesh: frame: 16 (over x_lo, y, core), tile: 16 (over z, x_hi).
Axes of the slice: x: 4 (x_hi: 2, x_lo: 2; x = x_hi * 2 + x_lo), y: 4, z: 8, core: 2. Of those that a mesh axis runs over, the one named last changes fastest.
Arguments:
- features: bfloat16 [16, 32, 16384], P('frame', None, 'tile'), may hold values from -6 to 6
- views: int32 [16, 4], replicated, may hold values from 0 to 15, as said below
- offsets: int32 [16, 4, 32, 128], P('frame', None, None, 'tile'), may hold values from -2 to 2
- kernels: bfloat16 [32, 128, 128], replicated, may hold values from -0.5 to 0.5
- reg_weight: bfloat16 [3, 8, 32], replicated, may hold values from -0.625 to 0.625
- head_weight: float32 [8], replicated, may hold values from -2 to 2
- depth_cot: float32 [16, 16384], P('frame', 'tile'), may hold values from -120 to 120
Outputs:
- depth: float32 [16, 16384], P('frame', 'tile')
- feature_grad: float32 [16, 32, 16384], P('frame', None, 'tile')
The draws below stay inside these ranges and needn't reach their ends.
Inputs may be any that keep to these rules, and one draw needn't show every extreme that they name: `views`: row f lists 4 different frames, none of them f.
All inputs are finite; a program needn't handle non-finite values.
Results may differ from the reference program's by a relative error of at most 0.017.
The reference program's roundings to bfloat16 on the way count: a program that leaves them out, or rounds other values in their place, can miss the bound.
Values may be sent and summed in bfloat16 or wider, within the bound.
A program may use at most 64 MiB of HBM per device.

```python
import jax
import jax.numpy as jnp
from jax import lax

C = 32
P_SIZE = 32
R = 8
V = 4
HB = 2
F = 16
NBLK = 128
PIX = 16384


def draw_views(key, part):
    scores = jax.random.randint(key, (F, F - 1), 0, 1 << 20)
    columns = jnp.arange(F - 1, dtype=jnp.int32)[None, :]
    frame_rows = jnp.arange(F, dtype=jnp.int32)[:, None]
    scores = scores * F + columns
    forced = (frame_rows == 0) & (columns == F - 2) | (frame_rows == F - 1) & (columns == 0)
    scores = jnp.where(forced, (1 << 20) * F + F, scores)
    chosen = lax.top_k(scores, V)[1]
    return ((frame_rows + 1 + chosen) % F).astype(jnp.int32)


def with_ends(values, key, least, high):
    spot = [jax.random.randint(jax.random.fold_in(key, axis), (), 0, length) for axis, length in enumerate(values.shape)]
    longest = values.shape.index(max(values.shape))
    next_to = spot[:longest] + [(spot[longest] + 1) % values.shape[longest]] + spot[longest + 1:]
    return values.at[tuple(spot)].set(least).at[tuple(next_to)].set(high)


def block_scale(stream_key, shape, pieces, smallest, top_value):
    level = 1.0
    for position, shards_of in pieces:
        steps = jax.random.uniform(jax.random.fold_in(jax.random.fold_in(stream_key, 6), position), (shards_of,), jnp.float32, smallest / len(pieces), top_value / len(pieces))
        level = level * jnp.repeat(jnp.exp(steps), shape[position] // shards_of).reshape((-1,) + (1,) * (len(shape) - 1 - position))
    return level


def noise(stream_key, shape, scale, most, shards=(), kind=jnp.bfloat16):
    values = scale * jax.random.normal(stream_key, shape, jnp.float32)
    if shards:
        values = values * block_scale(stream_key, shape, shards, -0.22, 0.18)
    return jnp.clip(values, -most, most).astype(kind)


def setup_inputs(seed: int = 0) -> dict:
    key_of = jax.random.split(jax.random.key(seed), 8)
    return {
        "features": noise(key_of[0], (F, C, PIX), 1.0, 6.0, ((0, 16), (2, 16))),
        "views": draw_views(jax.random.fold_in(key_of[7], 71), 0),
        "offsets": with_ends(jax.random.randint(key_of[2], (F, V, P_SIZE, NBLK), -HB, HB + 1), jax.random.fold_in(key_of[2], 1), -HB, HB).astype(jnp.int32),
        "kernels": noise(key_of[3], (P_SIZE, 128, 128), 128 ** -0.5, 0.5),
        "reg_weight": noise(key_of[4], (3, R, C), (3 * C) ** -0.5, 0.625),
        "head_weight": noise(key_of[5], (R,), R ** -0.5, 2.0, (), jnp.float32),
        "depth_cot": noise(key_of[6], (F, PIX), 20.0, 120.0, ((0, 16), (1, 16)), jnp.float32),
    }


def warp_plane(reference_feat, sources, shifts, kernel):
    vcount, channels, pixels = sources.shape
    block_count = pixels // 128
    blocks = sources.reshape(vcount, channels, block_count, 128)
    target = jnp.arange(block_count, dtype=jnp.int32)[None, :] + shifts
    inside = (target >= 0) & (target < block_count)
    clipped = jnp.clip(target, 0, block_count - 1).astype(jnp.int32)
    picked = jax.vmap(lambda blockset, where_at: jnp.take(blockset, where_at, axis=1))(blocks, clipped)
    picked = jnp.where(inside[:, None, :, None], picked, 0.0).astype(jnp.bfloat16)
    warped = jnp.dot(picked.reshape(-1, 128), kernel, preferred_element_type=jnp.float32)
    warped = warped.reshape(vcount, channels, pixels)
    stacked = jnp.concatenate([reference_feat[None], warped], axis=0)
    average = lax.optimization_barrier(jnp.sum(stacked, axis=0)) / (V + 1)
    centred = stacked - average[None]
    return (lax.optimization_barrier(jnp.sum(centred * centred, axis=0)) / (V + 1)).astype(jnp.bfloat16)

def regularize(volume, reg_weight, head_weight):
    planes = volume.astype(jnp.float32)
    padded = jnp.pad(planes, ((1, 1), (0, 0), (0, 0)))
    hidden = jnp.einsum('rc,dcp->drp', reg_weight[0].astype(jnp.float32), padded[0:P_SIZE])
    for tap_index in range(1, 3):
        hidden = hidden + jnp.einsum('rc,dcp->drp', reg_weight[tap_index].astype(jnp.float32), padded[tap_index:tap_index + P_SIZE])
    scores = 4.0 * jnp.tanh(lax.optimization_barrier(jnp.sum(hidden * head_weight[None, :, None], axis=1)))
    weights = jnp.exp(scores)
    values = (jnp.arange(P_SIZE, dtype=jnp.float32) + 1.0) / P_SIZE
    return lax.optimization_barrier(jnp.sum(weights * values[:, None], axis=0)) / lax.optimization_barrier(jnp.sum(weights, axis=0))

def reference(features, views, offsets, kernels, reg_weight, head_weight, depth_cot):

    def all_depth(feat_copy):

        def one_frame(frame_id):
            reference_feat = feat_copy[frame_id]
            sources = feat_copy[views[frame_id]]
            shifts = jnp.transpose(offsets[frame_id], (1, 0, 2))

            def per_plane(plane_items):
                return warp_plane(reference_feat, sources, plane_items[0], plane_items[1])
            volume = lax.map(jax.checkpoint(per_plane), (shifts, kernels))
            return regularize(volume, reg_weight, head_weight)
        return lax.map(jax.checkpoint(one_frame), jnp.arange(F, dtype=jnp.int32))
    feat_copy = features.astype(jnp.float32)
    depth_map, pullback = jax.vjp(all_depth, feat_copy)
    feature_grad = pullback(depth_cot)[0]
    return (depth_map, feature_grad)
```

```python
import functools

import jax
import jax.numpy as jnp
from jax import lax
from jax.experimental import pallas as pl
from jax.experimental.pallas import tpu as pltpu
from jax.sharding import PartitionSpec as P

MESH = pl.DeviceIdType.MESH
f32, bf16, i32 = jnp.float32, jnp.bfloat16, jnp.int32

C = 32
D = 32
V = 4
NF = 8
NB = 8
W = 5
ZERO = 2 * NF * W

PARTS = ((0, 0, 2, 3), (1, 1, 1, 4), (2, 5, 0, 5), (6, 6, 0, 4), (7, 7, 0, 3))


def place():
    frame = lax.axis_index("frame")
    tile = lax.axis_index("tile")
    core = frame % 2
    own = frame // 2
    return frame, core, own, (own % 4) * 2 + own // 4, tile, lax.axis_size("tile")


def frame_at(block, core):
    return (block % 2) * 8 + (block // 2) * 2 + core


def signal(semaphore, frame, tile):
    pl.semaphore_signal(semaphore, inc=1, device_id=(frame, tile), device_id_type=MESH)


def remote(src, dst, send, recv, frame, tile):
    return pltpu.make_async_remote_copy(
        src_ref=src, dst_ref=dst, send_sem=send, recv_sem=recv, device_id=(frame, tile), device_id_type=MESH
    )


def wait_bytes(ref, semaphore):
    pltpu.make_async_copy(ref, ref, semaphore).wait()


def exchange_kernel(
    feats, offsets, cot, views, win, index_out, cot_out,
    blocks, aux, aux_rx, send, recv, aux_send, aux_recv, rim_send, sib_send, sib_recv,
):
    frame, core, own, mine, tile, tiles = place()
    before, after = (tile + tiles - 1) % tiles, (tile + 1) % tiles
    sibling = frame + 1 - 2 * core

    barrier = pltpu.get_barrier_semaphore()

    def greet(s, carry):
        signal(barrier, frame_at((mine + s) % NB, core), tile)
        return carry

    lax.fori_loop(1, NB, greet, 0)

    @pl.when(mine < 2)
    def _():
        def greet_before(b, carry):
            signal(barrier, frame_at(b, core), before)
            return carry

        lax.fori_loop(0, NB, greet_before, 0)

    @pl.when(mine > 5)
    def _():
        def greet_after(b, carry):
            signal(barrier, frame_at(b, core), after)
            return carry

        lax.fori_loop(0, NB, greet_after, 0)

    signal(barrier, sibling, tile)

    for b in range(NB):
        blocks[b] = feats[:, b * 128:(b + 1) * 128]
        for j in range(V):
            aux[b, :, j * D:(j + 1) * D] = offsets[j, b:b + 1, :].astype(f32)
        aux[b, :, 128:256] = cot[:, b * 128:(b + 1) * 128]
    win[ZERO] = jnp.zeros((C, 128), bf16)

    pl.semaphore_wait(barrier, 7 + 4 + 1)

    rims = (
        (0, 1, 4, 6, before), (0, 2, 3, 7, before),
        (6, 2, 0, 0, after), (7, 1, 0, 1, after),
    )
    rim_copies = [
        remote(
            blocks.at[pl.ds(first, count)], win.at[pl.ds(own * W + at, count)],
            rim_send.at[n], recv.at[own], frame_at(b, core), where,
        )
        for n, (first, count, at, b, where) in enumerate(rims)
    ]
    for copy in rim_copies:
        copy.start()

    def part_copy(b, at, count):
        return remote(
            blocks.at[pl.ds(b - 2 + at, count)], win.at[pl.ds(own * W + at, count)],
            send.at[b], recv.at[own], frame_at(b, core), tile,
        )

    def aux_copy(b):
        return remote(aux.at[b], aux_rx.at[own], aux_send.at[b], aux_recv.at[own], frame_at(b, core), tile)

    def start(s, carry):
        b = (mine + s) % NB
        aux_copy(b).start()
        for least, most, at, count in PARTS:
            @pl.when((b >= least) & (b <= most))
            def _():
                part_copy(b, at, count).start()
        return carry

    lax.fori_loop(1, NB, start, 0)
    pltpu.make_async_copy(aux.at[mine], aux_rx.at[own], aux_recv.at[own]).start()
    for least, most, at, count in PARTS:
        @pl.when((mine >= least) & (mine <= most))
        def _():
            pltpu.make_async_copy(
                blocks.at[pl.ds(mine - 2 + at, count)], win.at[pl.ds(own * W + at, count)], recv.at[own]
            ).start()

    def window(i):
        return win.at[pl.ds(i * W, W)]

    def to_sibling(i):
        return remote(
            window(i), window(NF + i), sib_send.at[i], sib_recv.at[i], sibling, tile
        )

    def forward(s, carry):
        i = (own + s) % NF
        wait_bytes(window(i), recv.at[i])
        to_sibling(i).start()
        return carry

    lax.fori_loop(0, NF, forward, 0)

    view_of = lax.broadcasted_iota(i32, (1, 128), 1) // D
    here = tile * NB + mine
    for i in range(NF):
        wait_bytes(aux_rx.at[i], aux_recv.at[i])
        shift = aux_rx[i, :, 0:128].astype(i32)
        at = here + shift
        row = jnp.zeros((1, 128), i32)
        for j in range(V):
            v = views[j, 2 * i + core]
            row = jnp.where(view_of == j, jnp.where(v % 2 == core, 0, NF * W) + (v // 2) * W + 2, row)
        index_out[i:i + 1, :] = jnp.where((at >= 0) & (at < tiles * NB), row + shift, ZERO)
        cot_out[i:i + 1, :] = aux_rx[i, :, 128:256]

    def settle(s, carry):
        b = (mine + s) % NB
        aux_copy(b).wait_send()
        for least, most, at, count in PARTS:
            @pl.when((b >= least) & (b <= most))
            def _():
                part_copy(b, at, count).wait_send()
        return carry

    lax.fori_loop(1, NB, settle, 0)
    for copy in rim_copies:
        copy.wait_send()

    def settle_sibling(i, carry):
        to_sibling(i).wait_send()
        wait_bytes(window(NF + i), sib_recv.at[i])
        return carry

    lax.fori_loop(0, NF, settle_sibling, 0)


def compute_kernel(
    idx, head, win, ker, reg, cot, depth_out, grad_own, grad_sib, cen, vd, acc_a, acc_b, ref_acc
):
    step = 2
    rows = []
    for t in range(3):
        taps = reg[t].astype(f32)
        rows.append(sum(head[r] * taps[r:r + 1, :] for r in range(8)))
    row_id = lax.broadcasted_iota(i32, (8, C), 0)
    weight = jnp.where(row_id == 0, rows[0], jnp.where(row_id == 1, rows[1], jnp.where(row_id == 2, rows[2], 0.0)))
    w_hi = weight.astype(bf16)
    w_lo = (weight - w_hi.astype(f32)).astype(bf16)
    wide_lane = lax.broadcasted_iota(i32, (C, D * C), 1)
    wide_row = lax.broadcasted_iota(i32, (C, D * C), 0)
    spread = (wide_lane % C == wide_row).astype(f32).astype(bf16)
    tap_of = wide_lane // C - wide_row + 1
    bands = []
    for part in (w_hi, w_lo):
        wide = jnp.dot(part, spread, preferred_element_type=f32)
        bands.append(sum(jnp.where(tap_of == t, wide[t:t + 1, :], 0.0) for t in range(3)))
    mean_of = 1.0 / (V + 1)

    def forward(d, carry):
        mat = ker[d]
        for i0 in range(0, NF, step):
            picks = [win[idx[i, j * D + d]] for i in range(i0, i0 + step) for j in range(V)]
            y = jnp.dot(jnp.concatenate(picks, axis=0), mat, preferred_element_type=f32)
            for i in range(i0, i0 + step):
                o = (i - i0) * V * C
                xs = [win[i * W + 2].astype(f32)] + [y[o + j * C:o + (j + 1) * C] for j in range(V)]
                average = (((xs[0] + xs[1]) + (xs[2] + xs[3])) + xs[4]) * mean_of
                cs = [x - average for x in xs]
                sq = [c * c for c in cs]
                variance = (((sq[0] + sq[1]) + (sq[2] + sq[3])) + sq[4]) * mean_of
                vd[pl.ds(pl.multiple_of(d * C, C), C), i * 128:(i + 1) * 128] = variance.astype(bf16)
                for j in range(V + 1):
                    cen[d, i, j] = cs[j].astype(bf16)
        return carry

    lax.fori_loop(0, D, forward, 0)

    band = jnp.concatenate(bands, axis=0).astype(bf16)
    band_t = jnp.transpose(jnp.concatenate(bands + bands, axis=0)).astype(bf16)
    value = (lax.broadcasted_iota(i32, (D, 128), 0).astype(f32) + 1.0) / D
    for i0 in range(0, NF, 2):
        both = jnp.dot(band, vd[:, i0 * 128:(i0 + 2) * 128], preferred_element_type=f32)
        parts = []
        for i in range(i0, i0 + 2):
            o = (i - i0) * 128
            th = jnp.tanh(both[:D, o:o + 128] + both[D:, o:o + 128])
            w = jnp.exp(4.0 * th)
            total = jnp.sum(w, axis=0, keepdims=True)
            depth = jnp.sum(w * value, axis=0, keepdims=True) / total
            depth_out[i:i + 1, :] = depth
            scale = cot[i:i + 1, :] / total * (4.0 * 2.0 / (V + 1))
            d_pre = (w * (value - depth)) * scale * (1.0 - th * th)
            hi = d_pre.astype(bf16)
            lo = (d_pre - hi.astype(f32)).astype(bf16)
            parts.append(jnp.concatenate([hi, hi, lo, lo], axis=0))
        rhs = jnp.concatenate(parts, axis=1)
        vd[:, i0 * 128:(i0 + 2) * 128] = jnp.dot(band_t, rhs, preferred_element_type=f32).astype(bf16)

    acc_a[...] = jnp.zeros_like(acc_a)
    acc_b[...] = jnp.zeros_like(acc_b)
    ref_acc[...] = jnp.zeros_like(ref_acc)

    def backward(d, carry):
        mat = ker[d]
        for i0 in range(0, NF, step):
            gs = []
            for i in range(i0, i0 + step):
                dv = vd[pl.ds(pl.multiple_of(d * C, C), C), i * 128:(i + 1) * 128]
                ref_acc[i] += (dv * cen[d, i, 0]).astype(f32)
                for j in range(V):
                    gs.append(dv * cen[d, i, j + 1])
            y = lax.dot_general(
                jnp.concatenate(gs, axis=0), mat, (((1,), (1,)), ((), ())), preferred_element_type=f32
            )
            for i in range(i0, i0 + step):
                acc = acc_a if i % 2 == 0 else acc_b
                slots = [idx[i, j * D + d] for j in range(V)]
                o = (i - i0) * V * C
                new = [acc[slots[j]] + y[o + j * C:o + (j + 1) * C] for j in range(V)]
                for j in range(V):
                    acc[slots[j]] = new[j]
        return carry

    lax.fori_loop(0, D, backward, 0)

    for i in range(NF):
        for k in range(W):
            s = i * W + k
            total = acc_a[s] + acc_b[s]
            grad_own[s] = total + ref_acc[i] if k == 2 else total
            grad_sib[s] = (acc_a[NF * W + s] + acc_b[NF * W + s]).astype(bf16)


def return_kernel(
    grad_own, grad_sib, depth, depth_out, grad_out,
    sib_rx, out, depths, depth_rx, rx, send, recv, rim_send, depth_send, depth_recv, sib_send, sib_recv,
):
    frame, core, own, mine, tile, tiles = place()
    before, after = (tile + tiles - 1) % tiles, (tile + 1) % tiles
    sibling = frame + 1 - 2 * core

    barrier = pltpu.get_barrier_semaphore()
    signal(barrier, sibling, tile)

    def greet(s, carry):
        signal(barrier, frame_at((mine + s) % NB, core), tile)
        return carry

    lax.fori_loop(1, NB, greet, 0)
    for b, where in ((6, before), (7, before), (0, after), (1, after)):
        signal(barrier, frame_at(b, core), where)
    for i in range(NF):
        depths[i] = depth[i:i + 1, :]

    pl.semaphore_wait(barrier, jnp.where((mine < 2) | (mine > 5), 2 * NB, NB))

    def window(ref, i):
        return ref.at[pl.ds(i * W, W)]

    def to_sibling(i):
        return remote(
            window(grad_sib, i), window(sib_rx, i), sib_send.at[i], sib_recv.at[i], sibling, tile
        )

    def start_sibling(s, carry):
        to_sibling((own + s) % NF).start()
        return carry

    lax.fori_loop(1, NF + 1, start_sibling, 0)

    def part_copy(i, at, count):
        return remote(
            out.at[pl.ds(i * W + at, count)], rx.at[mine + 2, pl.ds(at, count)],
            send.at[i], recv.at[mine + 2], 2 * i + core, tile,
        )

    def rim_copy(i, at, count, slot, where):
        return remote(
            out.at[pl.ds(i * W + at, count)], rx.at[slot, pl.ds(at, count)],
            rim_send.at[i], recv.at[slot], 2 * i + core, where,
        )

    def depth_copy(i):
        return remote(
            depths.at[i], depth_rx.at[mine], depth_send.at[i], depth_recv.at[mine], 2 * i + core, tile
        )

    rims = ((0, 0, 2, 10, before), (1, 0, 1, 11, before), (6, 4, 1, 0, after), (7, 3, 2, 1, after))

    def add_and_send(s, carry):
        i = (own + s) % NF
        wait_bytes(window(sib_rx, i), sib_recv.at[i])
        for k in range(W):
            out[i * W + k] = (grad_own[i * W + k] + sib_rx[i * W + k].astype(f32)).astype(bf16)
        for b, at, count, slot, where in rims:
            @pl.when(mine == b)
            def _():
                rim_copy(i, at, count, slot, where).start()

        @pl.when(i != own)
        def _():
            depth_copy(i).start()
            for least, most, at, count in PARTS:
                @pl.when((mine >= least) & (mine <= most))
                def _():
                    part_copy(i, at, count).start()

        return carry

    lax.fori_loop(1, NF + 1, add_and_send, 0)
    pltpu.make_async_copy(depths.at[own], depth_rx.at[mine], depth_recv.at[mine]).start()
    for least, most, at, count in PARTS:
        @pl.when((mine >= least) & (mine <= most))
        def _():
            pltpu.make_async_copy(
                out.at[pl.ds(own * W + at, count)], rx.at[mine + 2, pl.ds(at, count)], recv.at[mine + 2]
            ).start()

    for b in range(NB):
        wait_bytes(depth_rx.at[b], depth_recv.at[b])
        depth_out[:, b * 128:(b + 1) * 128] = depth_rx[b]
    for slot in range(NB + 4):
        first, last = max(slot - 4, 0), min(slot, NB - 1)
        wait_bytes(rx.at[slot, pl.ds(first - slot + 4, last - first + 1)], recv.at[slot])
    for b in range(NB):
        total = rx[b, 4].astype(f32)
        for k in range(1, W):
            total += rx[b + k, 4 - k].astype(f32)
        grad_out[:, b * 128:(b + 1) * 128] = total

    def settle(s, carry):
        i = (own + s) % NF
        to_sibling(i).wait_send()
        for b, at, count, slot, where in rims:
            @pl.when(mine == b)
            def _():
                rim_copy(i, at, count, slot, where).wait_send()

        @pl.when(i != own)
        def _():
            depth_copy(i).wait_send()
            for least, most, at, count in PARTS:
                @pl.when((mine >= least) & (mine <= most))
                def _():
                    part_copy(i, at, count).wait_send()

        return carry

    lax.fori_loop(1, NF + 1, settle, 0)


def per_device(features, views, offsets, kernels, reg_weight, head_weight, depth_cot):
    vmem = pl.BlockSpec(memory_space=pltpu.VMEM)
    smem = pl.BlockSpec(memory_space=pltpu.SMEM)
    dma = pltpu.SemaphoreType.DMA
    shape = jax.ShapeDtypeStruct

    win, index, cot = pl.pallas_call(
        exchange_kernel,
        name="exchange",
        out_shape=(shape((ZERO + 1, C, 128), bf16), shape((NF, 128), i32), shape((NF, 128), f32)),
        in_specs=[vmem, vmem, vmem, smem],
        out_specs=(vmem,) * 3,
        scratch_shapes=[
            pltpu.VMEM((NB, C, 128), bf16),
            pltpu.VMEM((NB, 1, 256), f32),
            pltpu.VMEM((NF, 1, 256), f32),
            dma((NB,)), dma((NF,)), dma((NB,)), dma((NF,)), dma((4,)), dma((NF,)), dma((NF,)),
        ],
        compiler_params=pltpu.CompilerParams(
            collective_id=0, has_side_effects=True, vmem_limit_bytes=16 << 20
        ),
    )(features.reshape(C, NB * 128), jnp.transpose(offsets[0], (0, 2, 1)), depth_cot, views.T)

    depth, grad_own, grad_sib = pl.pallas_call(
        compute_kernel,
        name="compute",
        out_shape=(shape((NF, 128), f32), shape((NF * W, C, 128), f32), shape((NF * W, C, 128), bf16)),
        in_specs=[smem, smem, vmem, vmem, vmem, vmem],
        out_specs=(vmem,) * 3,
        scratch_shapes=[
            pltpu.VMEM((D, NF, V + 1, C, 128), bf16),
            pltpu.VMEM((D * C, NF * 128), bf16),
            pltpu.VMEM((ZERO + 1, C, 128), f32),
            pltpu.VMEM((ZERO + 1, C, 128), f32),
            pltpu.VMEM((NF, C, 128), f32),
        ],
        compiler_params=pltpu.CompilerParams(vmem_limit_bytes=40 << 20),
    )(index, head_weight, win, kernels, reg_weight, cot)

    depth_map, grad = pl.pallas_call(
        return_kernel,
        name="give_back",
        out_shape=(shape((1, NB * 128), f32), shape((C, NB * 128), f32)),
        in_specs=[vmem] * 3,
        out_specs=(vmem,) * 2,
        scratch_shapes=[
            pltpu.VMEM((NF * W, C, 128), bf16),
            pltpu.VMEM((NF * W, C, 128), bf16),
            pltpu.VMEM((NF, 1, 128), f32),
            pltpu.VMEM((NB, 1, 128), f32),
            pltpu.VMEM((NB + 4, W, C, 128), bf16),
            dma((NF,)), dma((NB + 4,)), dma((NF,)), dma((NF,)), dma((NB,)), dma((NF,)), dma((NF,)),
        ],
        compiler_params=pltpu.CompilerParams(
            collective_id=1, has_side_effects=True, vmem_limit_bytes=16 << 20
        ),
    )(grad_own, grad_sib, depth)
    return depth_map, grad.reshape(1, C, NB * 128)


def solution(mesh):
    return jax.shard_map(
        per_device,
        mesh=mesh,
        in_specs=(
            P("frame", None, "tile"),
            P(),
            P("frame", None, None, "tile"),
            P(),
            P(),
            P(),
            P("frame", "tile"),
        ),
        out_specs=(P("frame", "tile"), P("frame", None, "tile")),
        check_vma=False,
    )
```

```python
import functools

import jax
import jax.numpy as jnp
from jax import lax
from jax.experimental import pallas as pl
from jax.experimental.pallas import tpu as pltpu
from jax.sharding import PartitionSpec as P

MESH = pl.DeviceIdType.MESH
f32, bf16, i32 = jnp.float32, jnp.bfloat16, jnp.int32

C = 32
D = 32
V = 4
NF = 8
NB = 8
W = 5
ZERO = 2 * NF * W

PARTS = ((0, 0, 2, 3), (1, 1, 1, 4), (2, 5, 0, 5), (6, 6, 0, 4), (7, 7, 0, 3))


def place():
    frame = lax.axis_index("frame")
    tile = lax.axis_index("tile")
    core = frame % 2
    own = frame // 2
    return frame, core, own, (own % 4) * 2 + own // 4, tile, lax.axis_size("tile")


def frame_at(block, core):
    return (block % 2) * 8 + (block // 2) * 2 + core


def signal(semaphore, frame, tile):
    pl.semaphore_signal(semaphore, inc=1, device_id=(frame, tile), device_id_type=MESH)


def remote(src, dst, send, recv, frame, tile):
    return pltpu.make_async_remote_copy(
        src_ref=src, dst_ref=dst, send_sem=send, recv_sem=recv, device_id=(frame, tile), device_id_type=MESH
    )


def wait_bytes(ref, semaphore):
    pltpu.make_async_copy(ref, ref, semaphore).wait()


def make_bands(taps, head, band, band_t):
    rows = []
    for t in range(3):
        tap = taps[t].astype(f32)
        rows.append(sum(head[r] * tap[r:r + 1, :] for r in range(8)))
    row_id = lax.broadcasted_iota(i32, (8, C), 0)
    weight = jnp.where(row_id == 0, rows[0], jnp.where(row_id == 1, rows[1], jnp.where(row_id == 2, rows[2], 0.0)))
    w_hi = weight.astype(bf16)
    w_lo = (weight - w_hi.astype(f32)).astype(bf16)
    wide_lane = lax.broadcasted_iota(i32, (C, D * C), 1)
    wide_row = lax.broadcasted_iota(i32, (C, D * C), 0)
    spread = (wide_lane % C == wide_row).astype(f32).astype(bf16)
    tap_of = wide_lane // C - wide_row + 1
    bands = []
    for part in (w_hi, w_lo):
        wide = jnp.dot(part, spread, preferred_element_type=f32)
        bands.append(sum(jnp.where(tap_of == t, wide[t:t + 1, :], 0.0) for t in range(3)))
    band[...] = jnp.concatenate(bands, axis=0).astype(bf16)
    band_t[...] = jnp.transpose(jnp.concatenate(bands + bands, axis=0)).astype(bf16)


def exchange_kernel(
    feats, offsets_hbm, cot_hbm, views_hbm, kernels, taps_hbm, head_hbm,
    win, index_out, cot_out, diag, band, band_t,
    blocks, offsets, cot, taps, views, head, aux, aux_rx,
    send, recv, aux_send, aux_recv, rim_send, sib_send, sib_recv, load,
):
    frame, core, own, mine, tile, tiles = place()
    before, after = (tile + tiles - 1) % tiles, (tile + 1) % tiles
    sibling = frame + 1 - 2 * core

    barrier = pltpu.get_barrier_semaphore()

    def greet(s, carry):
        signal(barrier, frame_at((mine + s) % NB, core), tile)
        return carry

    lax.fori_loop(1, NB, greet, 0)

    @pl.when(mine < 2)
    def _():
        def greet_before(b, carry):
            signal(barrier, frame_at(b, core), before)
            return carry

        lax.fori_loop(0, NB, greet_before, 0)

    @pl.when(mine > 5)
    def _():
        def greet_after(b, carry):
            signal(barrier, frame_at(b, core), after)
            return carry

        lax.fori_loop(0, NB, greet_after, 0)

    signal(barrier, sibling, tile)

    for b in range(NB):
        pltpu.make_async_copy(feats.at[:, pl.ds(b * 128, 128)], blocks.at[b], load.at[0]).start()
    small = [
        pltpu.make_async_copy(src, dst, load.at[n])
        for n, (src, dst) in enumerate(
            ((offsets_hbm, offsets), (cot_hbm, cot), (views_hbm, views), (taps_hbm, taps), (head_hbm, head)), 1
        )
    ]
    half = [
        pltpu.make_async_copy(
            kernels.at[:, h], diag.at[:, pl.ds(h * 128, 128), pl.ds(h * 128, 128)], load.at[6 + h]
        )
        for h in range(2)
    ]
    for copy in small:
        copy.start()
    for copy in half:
        copy.start()
    win[ZERO] = jnp.zeros((C, 128), bf16)
    small[0].wait()
    small[1].wait()
    for b in range(NB):
        for j in range(V):
            aux[b, :, j * D:(j + 1) * D] = offsets[j, b:b + 1, :].astype(f32)
        aux[b, :, 128:256] = cot[:, b * 128:(b + 1) * 128]
    wait_bytes(blocks, load.at[0])

    pl.semaphore_wait(barrier, 7 + 4 + 1)

    rims = (
        (0, 1, 4, 6, before), (0, 2, 3, 7, before),
        (6, 2, 0, 0, after), (7, 1, 0, 1, after),
    )
    rim_copies = [
        remote(
            blocks.at[pl.ds(first, count)], win.at[pl.ds(own * W + at, count)],
            rim_send.at[n], recv.at[own], frame_at(b, core), where,
        )
        for n, (first, count, at, b, where) in enumerate(rims)
    ]
    for copy in rim_copies:
        copy.start()

    def part_copy(b, at, count):
        return remote(
            blocks.at[pl.ds(b - 2 + at, count)], win.at[pl.ds(own * W + at, count)],
            send.at[b], recv.at[own], frame_at(b, core), tile,
        )

    def aux_copy(b):
        return remote(aux.at[b], aux_rx.at[own], aux_send.at[b], aux_recv.at[own], frame_at(b, core), tile)

    def start(s, carry):
        b = (mine + s) % NB
        aux_copy(b).start()
        for least, most, at, count in PARTS:
            @pl.when((b >= least) & (b <= most))
            def _():
                part_copy(b, at, count).start()
        return carry

    lax.fori_loop(1, NB, start, 0)
    pltpu.make_async_copy(aux.at[mine], aux_rx.at[own], aux_recv.at[own]).start()
    for least, most, at, count in PARTS:
        @pl.when((mine >= least) & (mine <= most))
        def _():
            pltpu.make_async_copy(
                blocks.at[pl.ds(mine - 2 + at, count)], win.at[pl.ds(own * W + at, count)], recv.at[own]
            ).start()

    corner = jnp.zeros((D // 2, 128, 128), bf16)
    diag[:, 0:128, 128:256] = corner
    diag[:, 128:256, 0:128] = corner

    def window(i):
        return win.at[pl.ds(i * W, W)]

    def to_sibling(i):
        return remote(
            window(i), window(NF + i), sib_send.at[i], sib_recv.at[i], sibling, tile
        )

    def forward(s, carry):
        i = (own + s) % NF
        wait_bytes(window(i), recv.at[i])
        to_sibling(i).start()
        return carry

    lax.fori_loop(0, NF, forward, 0)

    for copy in small[2:]:
        copy.wait()
    make_bands(taps, head, band, band_t)

    view_of = lax.broadcasted_iota(i32, (1, 128), 1) // D
    here = tile * NB + mine
    for i in range(NF):
        wait_bytes(aux_rx.at[i], aux_recv.at[i])
        shift = aux_rx[i, :, 0:128].astype(i32)
        at = here + shift
        row = jnp.zeros((1, 128), i32)
        for j in range(V):
            v = views[j, 2 * i + core]
            row = jnp.where(view_of == j, jnp.where(v % 2 == core, 0, NF * W) + (v // 2) * W + 2, row)
        index_out[i:i + 1, :] = jnp.where((at >= 0) & (at < tiles * NB), row + shift, ZERO)
        cot_out[i:i + 1, :] = aux_rx[i, :, 128:256]

    def settle(s, carry):
        b = (mine + s) % NB
        aux_copy(b).wait_send()
        for least, most, at, count in PARTS:
            @pl.when((b >= least) & (b <= most))
            def _():
                part_copy(b, at, count).wait_send()
        return carry

    lax.fori_loop(1, NB, settle, 0)
    for copy in rim_copies:
        copy.wait_send()

    def settle_sibling(i, carry):
        to_sibling(i).wait_send()
        wait_bytes(window(NF + i), sib_recv.at[i])
        return carry

    lax.fori_loop(0, NF, settle_sibling, 0)
    for copy in half:
        copy.wait()


def compute_kernel(
    idx, win, diag, band, band_t, cot, depth_out, grad_own, grad_sib, cen, vd, acc_a, acc_b, ref_acc
):
    step = 2
    mean_of = 1.0 / (V + 1)

    def forward(p, carry):
        mat = diag[p]
        for i0 in range(0, NF, step):
            picks = [
                jnp.concatenate([win[idx[i, j * D + 2 * p + h]] for h in range(2)], axis=1)
                for i in range(i0, i0 + step) for j in range(V)
            ]
            y = jnp.dot(jnp.concatenate(picks, axis=0), mat, preferred_element_type=f32)
            for i in range(i0, i0 + step):
              for h in range(2):
                o = (i - i0) * V * C
                xs = [win[i * W + 2].astype(f32)] + [y[o + j * C:o + (j + 1) * C, h * 128:(h + 1) * 128] for j in range(V)]
                average = (((xs[0] + xs[1]) + (xs[2] + xs[3])) + xs[4]) * mean_of
                cs = [x - average for x in xs]
                sq = [c * c for c in cs]
                variance = (((sq[0] + sq[1]) + (sq[2] + sq[3])) + sq[4]) * mean_of
                d = 2 * p + h
                vd[pl.ds(pl.multiple_of(d * C, C), C), i * 128:(i + 1) * 128] = variance.astype(bf16)
                for j in range(V + 1):
                    cen[d, i, j] = cs[j].astype(bf16)
        return carry

    lax.fori_loop(0, D // 2, forward, 0)

    value = (lax.broadcasted_iota(i32, (D, 128), 0).astype(f32) + 1.0) / D
    for i0 in range(0, NF, 2):
        both = jnp.dot(band[...], vd[:, i0 * 128:(i0 + 2) * 128], preferred_element_type=f32)
        parts = []
        for i in range(i0, i0 + 2):
            o = (i - i0) * 128
            th = jnp.tanh(both[:D, o:o + 128] + both[D:, o:o + 128])
            w = jnp.exp(4.0 * th)
            total = jnp.sum(w, axis=0, keepdims=True)
            depth = jnp.sum(w * value, axis=0, keepdims=True) / total
            depth_out[i:i + 1, :] = depth
            scale = cot[i:i + 1, :] / total * (4.0 * 2.0 / (V + 1))
            d_pre = (w * (value - depth)) * scale * (1.0 - th * th)
            hi = d_pre.astype(bf16)
            lo = (d_pre - hi.astype(f32)).astype(bf16)
            parts.append(jnp.concatenate([hi, hi, lo, lo], axis=0))
        rhs = jnp.concatenate(parts, axis=1)
        vd[:, i0 * 128:(i0 + 2) * 128] = jnp.dot(band_t[...], rhs, preferred_element_type=f32).astype(bf16)

    acc_a[...] = jnp.zeros_like(acc_a)
    acc_b[...] = jnp.zeros_like(acc_b)
    ref_acc[...] = jnp.zeros_like(ref_acc)

    def backward(p, carry):
        mat = diag[p]
        for i0 in range(0, NF, step):
            gs = []
            for i in range(i0, i0 + step):
                dvs = [vd[pl.ds(pl.multiple_of((2 * p + h) * C, C), C), i * 128:(i + 1) * 128] for h in range(2)]
                ref_acc[i] += (dvs[0] * cen[2 * p, i, 0]).astype(f32) + (dvs[1] * cen[2 * p + 1, i, 0]).astype(f32)
                for j in range(V):
                    gs.append(jnp.concatenate([dvs[h] * cen[2 * p + h, i, j + 1] for h in range(2)], axis=1))
            y = lax.dot_general(
                jnp.concatenate(gs, axis=0), mat, (((1,), (1,)), ((), ())), preferred_element_type=f32
            )
            for h in range(2):
              for i in range(i0, i0 + step):
                acc = acc_a if i % 2 == 0 else acc_b
                slots = [idx[i, j * D + 2 * p + h] for j in range(V)]
                o = (i - i0) * V * C
                new = [acc[slots[j]] + y[o + j * C:o + (j + 1) * C, h * 128:(h + 1) * 128] for j in range(V)]
                for j in range(V):
                    acc[slots[j]] = new[j]
        return carry

    lax.fori_loop(0, D // 2, backward, 0)

    for i in range(NF):
        for k in range(W):
            s = i * W + k
            total = acc_a[s] + acc_b[s]
            grad_own[s] = total + ref_acc[i] if k == 2 else total
            grad_sib[s] = (acc_a[NF * W + s] + acc_b[NF * W + s]).astype(bf16)


def return_kernel(
    grad_own, grad_sib, depth, depth_out, grad_out,
    sib_rx, out, depths, depth_rx, rx, send, recv, rim_send, depth_send, depth_recv, sib_send, sib_recv,
):
    frame, core, own, mine, tile, tiles = place()
    before, after = (tile + tiles - 1) % tiles, (tile + 1) % tiles
    sibling = frame + 1 - 2 * core

    barrier = pltpu.get_barrier_semaphore()
    signal(barrier, sibling, tile)

    def greet(s, carry):
        signal(barrier, frame_at((mine + s) % NB, core), tile)
        return carry

    lax.fori_loop(1, NB, greet, 0)
    for b, where in ((6, before), (7, before), (0, after), (1, after)):
        signal(barrier, frame_at(b, core), where)
    for i in range(NF):
        depths[i] = depth[i:i + 1, :]

    pl.semaphore_wait(barrier, jnp.where((mine < 2) | (mine > 5), 2 * NB, NB))

    def window(ref, i):
        return ref.at[pl.ds(i * W, W)]

    def to_sibling(i):
        return remote(
            window(grad_sib, i), window(sib_rx, i), sib_send.at[i], sib_recv.at[i], sibling, tile
        )

    def start_sibling(s, carry):
        to_sibling((own + s) % NF).start()
        return carry

    lax.fori_loop(1, NF + 1, start_sibling, 0)

    def part_copy(i, at, count):
        return remote(
            out.at[pl.ds(i * W + at, count)], rx.at[mine + 2, pl.ds(at, count)],
            send.at[i], recv.at[mine + 2], 2 * i + core, tile,
        )

    def rim_copy(i, at, count, slot, where):
        return remote(
            out.at[pl.ds(i * W + at, count)], rx.at[slot, pl.ds(at, count)],
            rim_send.at[i], recv.at[slot], 2 * i + core, where,
        )

    def depth_copy(i):
        return remote(
            depths.at[i], depth_rx.at[mine], depth_send.at[i], depth_recv.at[mine], 2 * i + core, tile
        )

    rims = ((0, 0, 2, 10, before), (1, 0, 1, 11, before), (6, 4, 1, 0, after), (7, 3, 2, 1, after))

    def add_and_send(s, carry):
        i = (own + s) % NF
        wait_bytes(window(sib_rx, i), sib_recv.at[i])
        for k in range(W):
            out[i * W + k] = (grad_own[i * W + k] + sib_rx[i * W + k].astype(f32)).astype(bf16)
        for b, at, count, slot, where in rims:
            @pl.when(mine == b)
            def _():
                rim_copy(i, at, count, slot, where).start()

        @pl.when(i != own)
        def _():
            depth_copy(i).start()
            for least, most, at, count in PARTS:
                @pl.when((mine >= least) & (mine <= most))
                def _():
                    part_copy(i, at, count).start()

        return carry

    lax.fori_loop(1, NF + 1, add_and_send, 0)
    pltpu.make_async_copy(depths.at[own], depth_rx.at[mine], depth_recv.at[mine]).start()
    for least, most, at, count in PARTS:
        @pl.when((mine >= least) & (mine <= most))
        def _():
            pltpu.make_async_copy(
                out.at[pl.ds(own * W + at, count)], rx.at[mine + 2, pl.ds(at, count)], recv.at[mine + 2]
            ).start()

    for b in range(NB):
        wait_bytes(depth_rx.at[b], depth_recv.at[b])
        depth_out[:, b * 128:(b + 1) * 128] = depth_rx[b]
    for slot in range(NB + 4):
        first, last = max(slot - 4, 0), min(slot, NB - 1)
        wait_bytes(rx.at[slot, pl.ds(first - slot + 4, last - first + 1)], recv.at[slot])
    for b in range(NB):
        total = rx[b, 4].astype(f32)
        for k in range(1, W):
            total += rx[b + k, 4 - k].astype(f32)
        grad_out[:, b * 128:(b + 1) * 128] = total

    def settle(s, carry):
        i = (own + s) % NF
        to_sibling(i).wait_send()
        for b, at, count, slot, where in rims:
            @pl.when(mine == b)
            def _():
                rim_copy(i, at, count, slot, where).wait_send()

        @pl.when(i != own)
        def _():
            depth_copy(i).wait_send()
            for least, most, at, count in PARTS:
                @pl.when((mine >= least) & (mine <= most))
                def _():
                    part_copy(i, at, count).wait_send()

        return carry

    lax.fori_loop(1, NF + 1, settle, 0)


def per_device(features, views, offsets, kernels, reg_weight, head_weight, depth_cot):
    vmem = pl.BlockSpec(memory_space=pltpu.VMEM)
    smem = pl.BlockSpec(memory_space=pltpu.SMEM)
    hbm = pl.BlockSpec(memory_space=pltpu.HBM)
    dma = pltpu.SemaphoreType.DMA
    shape = jax.ShapeDtypeStruct

    win, index, cot, diag, band, band_t = pl.pallas_call(
        exchange_kernel,
        name="exchange",
        out_shape=(
            shape((ZERO + 1, C, 128), bf16), shape((NF, 128), i32), shape((NF, 128), f32),
            shape((D // 2, 256, 256), bf16), shape((2 * D, D * C), bf16), shape((D * C, 4 * D), bf16),
        ),
        in_specs=[hbm] * 7,
        out_specs=(vmem,) * 6,
        scratch_shapes=[
            pltpu.VMEM((NB, C, 128), bf16),
            pltpu.VMEM((V, NB, D), i32),
            pltpu.VMEM((1, NB * 128), f32),
            pltpu.VMEM((3, 8, C), bf16),
            pltpu.SMEM((V, 16), i32),
            pltpu.SMEM((8,), f32),
            pltpu.VMEM((NB, 1, 256), f32),
            pltpu.VMEM((NF, 1, 256), f32),
            dma((NB,)), dma((NF,)), dma((NB,)), dma((NF,)), dma((4,)), dma((NF,)), dma((NF,)), dma((8,)),
        ],
        compiler_params=pltpu.CompilerParams(
            collective_id=0, has_side_effects=True, vmem_limit_bytes=16 << 20
        ),
    )(
        *(
            pltpu.with_memory_space_constraint(x, pltpu.HBM)
            for x in (
                features.reshape(C, NB * 128), jnp.transpose(offsets[0], (0, 2, 1)), depth_cot, views.T,
                kernels.reshape(D // 2, 2, 128, 128), reg_weight, head_weight,
            )
        )
    )

    depth, grad_own, grad_sib = pl.pallas_call(
        compute_kernel,
        name="compute",
        out_shape=(shape((NF, 128), f32), shape((NF * W, C, 128), f32), shape((NF * W, C, 128), bf16)),
        in_specs=[smem] + [vmem] * 5,
        out_specs=(vmem,) * 3,
        scratch_shapes=[
            pltpu.VMEM((D, NF, V + 1, C, 128), bf16),
            pltpu.VMEM((D * C, NF * 128), bf16),
            pltpu.VMEM((ZERO + 1, C, 128), f32),
            pltpu.VMEM((ZERO + 1, C, 128), f32),
            pltpu.VMEM((NF, C, 128), f32),
        ],
        compiler_params=pltpu.CompilerParams(vmem_limit_bytes=40 << 20),
    )(index, win, diag, band, band_t, cot)

    depth_map, grad = pl.pallas_call(
        return_kernel,
        name="give_back",
        out_shape=(shape((1, NB * 128), f32), shape((C, NB * 128), f32)),
        in_specs=[vmem] * 3,
        out_specs=(vmem,) * 2,
        scratch_shapes=[
            pltpu.VMEM((NF * W, C, 128), bf16),
            pltpu.VMEM((NF * W, C, 128), bf16),
            pltpu.VMEM((NF, 1, 128), f32),
            pltpu.VMEM((NB, 1, 128), f32),
            pltpu.VMEM((NB + 4, W, C, 128), bf16),
            dma((NF,)), dma((NB + 4,)), dma((NF,)), dma((NF,)), dma((NB,)), dma((NF,)), dma((NF,)),
        ],
        compiler_params=pltpu.CompilerParams(
            collective_id=1, has_side_effects=True, vmem_limit_bytes=16 << 20
        ),
    )(grad_own, grad_sib, depth)
    return depth_map, grad.reshape(1, C, NB * 128)


def solution(mesh):
    return jax.shard_map(
        per_device,
        mesh=mesh,
        in_specs=(
            P("frame", None, "tile"),
            P(),
            P("frame", None, None, "tile"),
            P(),
            P(),
            P(),
            P("frame", "tile"),
        ),
        out_specs=(P("frame", "tile"), P("frame", None, "tile")),
        check_vma=False,
    )
```

```python
import functools

import jax
import jax.numpy as jnp
from jax import lax
from jax.experimental import pallas as pl
from jax.experimental.pallas import tpu as pltpu
from jax.sharding import PartitionSpec as P

MESH = pl.DeviceIdType.MESH
f32, bf16, i32 = jnp.float32, jnp.bfloat16, jnp.int32

C = 32
D = 32
V = 4
NF = 8
NB = 8
W = 5
ZERO = 2 * NF * W

PARTS = ((0, 0, 2, 3), (1, 1, 1, 4), (2, 5, 0, 5), (6, 6, 0, 4), (7, 7, 0, 3))


def place():
    frame = lax.axis_index("frame")
    tile = lax.axis_index("tile")
    core = frame % 2
    own = frame // 2
    return frame, core, own, (own % 4) * 2 + own // 4, tile, lax.axis_size("tile")


def frame_at(block, core):
    return (block % 2) * 8 + (block // 2) * 2 + core


def signal(semaphore, frame, tile):
    pl.semaphore_signal(semaphore, inc=1, device_id=(frame, tile), device_id_type=MESH)


def remote(src, dst, send, recv, frame, tile):
    return pltpu.make_async_remote_copy(
        src_ref=src, dst_ref=dst, send_sem=send, recv_sem=recv, device_id=(frame, tile), device_id_type=MESH
    )


def wait_bytes(ref, semaphore):
    pltpu.make_async_copy(ref, ref, semaphore).wait()


def make_bands(taps, head, band, band_t):
    rows = []
    for t in range(3):
        tap = taps[t].astype(f32)
        rows.append(sum(head[r] * tap[r:r + 1, :] for r in range(8)))
    row_id = lax.broadcasted_iota(i32, (8, C), 0)
    weight = jnp.where(row_id == 0, rows[0], jnp.where(row_id == 1, rows[1], jnp.where(row_id == 2, rows[2], 0.0)))
    w_hi = weight.astype(bf16)
    w_lo = (weight - w_hi.astype(f32)).astype(bf16)
    wide_lane = lax.broadcasted_iota(i32, (C, D * C), 1)
    wide_row = lax.broadcasted_iota(i32, (C, D * C), 0)
    spread = (wide_lane % C == wide_row).astype(f32).astype(bf16)
    tap_of = wide_lane // C - wide_row + 1
    bands = []
    for part in (w_hi, w_lo):
        wide = jnp.dot(part, spread, preferred_element_type=f32)
        bands.append(sum(jnp.where(tap_of == t, wide[t:t + 1, :], 0.0) for t in range(3)))
    band[...] = jnp.concatenate(bands, axis=0).astype(bf16)
    band_t[...] = jnp.transpose(jnp.concatenate(bands + bands, axis=0)).astype(bf16)


def exchange_kernel(
    feats, offsets_hbm, cot_hbm, views_hbm, kernels, taps_hbm, head_hbm,
    win, index_out, cot_out, diag, band, band_t,
    blocks, offsets, cot, taps, views, head, aux, aux_rx,
    send, recv, aux_send, aux_recv, rim_send, sib_send, sib_recv, load,
):
    frame, core, own, mine, tile, tiles = place()
    before, after = (tile + tiles - 1) % tiles, (tile + 1) % tiles
    sibling = frame + 1 - 2 * core

    barrier = pltpu.get_barrier_semaphore()

    def greet(s, carry):
        signal(barrier, frame_at((mine + s) % NB, core), tile)
        return carry

    lax.fori_loop(1, NB, greet, 0)

    has_before, has_after = tile > 0, tile < tiles - 1
    edge = ((mine < 2) & (tile == 0)) | ((mine > 5) & (tile == tiles - 1))

    @pl.when((mine < 2) & has_before)
    def _():
        def greet_before(b, carry):
            signal(barrier, frame_at(b, core), before)
            return carry

        lax.fori_loop(0, NB, greet_before, 0)

    @pl.when((mine > 5) & has_after)
    def _():
        def greet_after(b, carry):
            signal(barrier, frame_at(b, core), after)
            return carry

        lax.fori_loop(0, NB, greet_after, 0)

    signal(barrier, sibling, tile)

    for b in range(NB):
        pltpu.make_async_copy(feats.at[:, pl.ds(b * 128, 128)], blocks.at[b], load.at[0]).start()
    small = [
        pltpu.make_async_copy(src, dst, load.at[n])
        for n, (src, dst) in enumerate(
            ((offsets_hbm, offsets), (cot_hbm, cot), (views_hbm, views), (taps_hbm, taps), (head_hbm, head)), 1
        )
    ]
    half = [
        pltpu.make_async_copy(
            kernels.at[:, h], diag.at[:, pl.ds(h * 128, 128), pl.ds(h * 128, 128)], load.at[6 + h]
        )
        for h in range(2)
    ]
    for copy in small:
        copy.start()
    for copy in half:
        copy.start()
    win[ZERO] = jnp.zeros((C, 128), bf16)
    for b, outside in ((0, (0, 1)), (1, (0,)), (6, (4,)), (7, (3, 4))):
        @pl.when((mine == b) & edge)
        def _():
            for i in range(NF):
                for k in outside:
                    win[i * W + k] = jnp.zeros((C, 128), bf16)

    small[0].wait()
    small[1].wait()
    for b in range(NB):
        for j in range(V):
            aux[b, :, j * D:(j + 1) * D] = offsets[j, b:b + 1, :].astype(f32)
        aux[b, :, 128:256] = cot[:, b * 128:(b + 1) * 128]
    wait_bytes(blocks, load.at[0])

    pl.semaphore_wait(barrier, NB + jnp.where(has_before, 2, 0) + jnp.where(has_after, 2, 0))

    rims = (
        (0, 1, 4, 6, before, has_before), (0, 2, 3, 7, before, has_before),
        (6, 2, 0, 0, after, has_after), (7, 1, 0, 1, after, has_after),
    )
    rim_copies = [
        (
            remote(
                blocks.at[pl.ds(first, count)], win.at[pl.ds(own * W + at, count)],
                rim_send.at[n], recv.at[own], frame_at(b, core), where,
            ),
            there,
        )
        for n, (first, count, at, b, where, there) in enumerate(rims)
    ]
    for copy, there in rim_copies:
        @pl.when(there)
        def _():
            copy.start()

    def part_copy(b, at, count):
        return remote(
            blocks.at[pl.ds(b - 2 + at, count)], win.at[pl.ds(own * W + at, count)],
            send.at[b], recv.at[own], frame_at(b, core), tile,
        )

    def aux_copy(b):
        return remote(aux.at[b], aux_rx.at[own], aux_send.at[b], aux_recv.at[own], frame_at(b, core), tile)

    def start(s, carry):
        b = (mine + s) % NB
        aux_copy(b).start()
        for least, most, at, count in PARTS:
            @pl.when((b >= least) & (b <= most))
            def _():
                part_copy(b, at, count).start()
        return carry

    lax.fori_loop(1, NB, start, 0)
    pltpu.make_async_copy(aux.at[mine], aux_rx.at[own], aux_recv.at[own]).start()
    for least, most, at, count in PARTS:
        @pl.when((mine >= least) & (mine <= most))
        def _():
            pltpu.make_async_copy(
                blocks.at[pl.ds(mine - 2 + at, count)], win.at[pl.ds(own * W + at, count)], recv.at[own]
            ).start()

    corner = jnp.zeros((D // 2, 128, 128), bf16)
    diag[:, 0:128, 128:256] = corner
    diag[:, 128:256, 0:128] = corner

    def window(i):
        return win.at[pl.ds(i * W, W)]

    def to_sibling(i):
        return remote(
            window(i), window(NF + i), sib_send.at[i], sib_recv.at[i], sibling, tile
        )

    def forward(s, carry):
        i = (own + s) % NF
        @pl.when(jnp.logical_not(edge))
        def _():
            wait_bytes(window(i), recv.at[i])

        for b, _, at, count in PARTS:
            if count < W:
                @pl.when((mine == b) & edge)
                def _():
                    wait_bytes(win.at[pl.ds(i * W + at, count)], recv.at[i])
        to_sibling(i).start()
        return carry

    lax.fori_loop(0, NF, forward, 0)

    for copy in small[2:]:
        copy.wait()
    make_bands(taps, head, band, band_t)

    view_of = lax.broadcasted_iota(i32, (1, 128), 1) // D
    here = tile * NB + mine
    for i in range(NF):
        wait_bytes(aux_rx.at[i], aux_recv.at[i])
        shift = aux_rx[i, :, 0:128].astype(i32)
        at = here + shift
        row = jnp.zeros((1, 128), i32)
        for j in range(V):
            v = views[j, 2 * i + core]
            row = jnp.where(view_of == j, jnp.where(v % 2 == core, 0, NF * W) + (v // 2) * W + 2, row)
        index_out[i:i + 1, :] = jnp.where((at >= 0) & (at < tiles * NB), row + shift, ZERO)
        cot_out[i:i + 1, :] = aux_rx[i, :, 128:256]

    def settle(s, carry):
        b = (mine + s) % NB
        aux_copy(b).wait_send()
        for least, most, at, count in PARTS:
            @pl.when((b >= least) & (b <= most))
            def _():
                part_copy(b, at, count).wait_send()
        return carry

    lax.fori_loop(1, NB, settle, 0)
    for copy, there in rim_copies:
        @pl.when(there)
        def _():
            copy.wait_send()

    def settle_sibling(i, carry):
        to_sibling(i).wait_send()
        wait_bytes(window(NF + i), sib_recv.at[i])
        return carry

    lax.fori_loop(0, NF, settle_sibling, 0)
    for copy in half:
        copy.wait()


def compute_kernel(
    idx, win, diag, band, band_t, cot, depth_out, grad_own, grad_sib, cen, vd, acc_a, acc_b, ref_acc
):
    step = 2
    mean_of = 1.0 / (V + 1)

    def forward(p, carry):
        mat = diag[p]
        for i0 in range(0, NF, step):
            picks = [
                jnp.concatenate([win[idx[i, j * D + 2 * p + h]] for h in range(2)], axis=1)
                for i in range(i0, i0 + step) for j in range(V)
            ]
            y = jnp.dot(jnp.concatenate(picks, axis=0), mat, preferred_element_type=f32)
            for i in range(i0, i0 + step):
              for h in range(2):
                o = (i - i0) * V * C
                xs = [win[i * W + 2].astype(f32)] + [y[o + j * C:o + (j + 1) * C, h * 128:(h + 1) * 128] for j in range(V)]
                average = (((xs[0] + xs[1]) + (xs[2] + xs[3])) + xs[4]) * mean_of
                cs = [x - average for x in xs]
                sq = [c * c for c in cs]
                variance = (((sq[0] + sq[1]) + (sq[2] + sq[3])) + sq[4]) * mean_of
                d = 2 * p + h
                vd[pl.ds(pl.multiple_of(d * C, C), C), i * 128:(i + 1) * 128] = variance.astype(bf16)
                for j in range(V + 1):
                    cen[d, i, j] = cs[j].astype(bf16)
        return carry

    lax.fori_loop(0, D // 2, forward, 0)

    value = (lax.broadcasted_iota(i32, (D, 128), 0).astype(f32) + 1.0) / D
    for i0 in range(0, NF, 2):
        both = jnp.dot(band[...], vd[:, i0 * 128:(i0 + 2) * 128], preferred_element_type=f32)
        parts = []
        for i in range(i0, i0 + 2):
            o = (i - i0) * 128
            th = jnp.tanh(both[:D, o:o + 128] + both[D:, o:o + 128])
            w = jnp.exp(4.0 * th)
            total = jnp.sum(w, axis=0, keepdims=True)
            depth = jnp.sum(w * value, axis=0, keepdims=True) / total
            depth_out[i:i + 1, :] = depth
            scale = cot[i:i + 1, :] / total * (4.0 * 2.0 / (V + 1))
            d_pre = (w * (value - depth)) * scale * (1.0 - th * th)
            hi = d_pre.astype(bf16)
            lo = (d_pre - hi.astype(f32)).astype(bf16)
            parts.append(jnp.concatenate([hi, hi, lo, lo], axis=0))
        rhs = jnp.concatenate(parts, axis=1)
        vd[:, i0 * 128:(i0 + 2) * 128] = jnp.dot(band_t[...], rhs, preferred_element_type=f32).astype(bf16)

    acc_a[...] = jnp.zeros_like(acc_a)
    acc_b[...] = jnp.zeros_like(acc_b)
    ref_acc[...] = jnp.zeros_like(ref_acc)

    def backward(p, carry):
        mat = diag[p]
        for i0 in range(0, NF, step):
            gs = []
            for i in range(i0, i0 + step):
                dvs = [vd[pl.ds(pl.multiple_of((2 * p + h) * C, C), C), i * 128:(i + 1) * 128] for h in range(2)]
                ref_acc[i] += (dvs[0] * cen[2 * p, i, 0]).astype(f32) + (dvs[1] * cen[2 * p + 1, i, 0]).astype(f32)
                for j in range(V):
                    gs.append(jnp.concatenate([dvs[h] * cen[2 * p + h, i, j + 1] for h in range(2)], axis=1))
            y = lax.dot_general(
                jnp.concatenate(gs, axis=0), mat, (((1,), (1,)), ((), ())), preferred_element_type=f32
            )
            for h in range(2):
              for i in range(i0, i0 + step):
                acc = acc_a if i % 2 == 0 else acc_b
                slots = [idx[i, j * D + 2 * p + h] for j in range(V)]
                o = (i - i0) * V * C
                new = [acc[slots[j]] + y[o + j * C:o + (j + 1) * C, h * 128:(h + 1) * 128] for j in range(V)]
                for j in range(V):
                    acc[slots[j]] = new[j]
        return carry

    lax.fori_loop(0, D // 2, backward, 0)

    for i in range(NF):
        for k in range(W):
            s = i * W + k
            total = acc_a[s] + acc_b[s]
            grad_own[s] = total + ref_acc[i] if k == 2 else total
            grad_sib[s] = (acc_a[NF * W + s] + acc_b[NF * W + s]).astype(bf16)


def return_kernel(
    grad_own, grad_sib, depth, depth_rx, rx,
    sib_rx, out, depths, send, recv, rim_send, depth_send, depth_recv, sib_send, sib_recv,
):
    frame, core, own, mine, tile, tiles = place()
    before, after = (tile + tiles - 1) % tiles, (tile + 1) % tiles
    sibling = frame + 1 - 2 * core

    barrier = pltpu.get_barrier_semaphore()
    signal(barrier, sibling, tile)

    def greet(s, carry):
        signal(barrier, frame_at((mine + s) % NB, core), tile)
        return carry

    lax.fori_loop(1, NB, greet, 0)
    has_before, has_after = tile > 0, tile < tiles - 1

    @pl.when(has_before)
    def _():
        for b in (6, 7):
            signal(barrier, frame_at(b, core), before)

    @pl.when(has_after)
    def _():
        for b in (0, 1):
            signal(barrier, frame_at(b, core), after)

    outer = [
        (slot, first - slot + 4, last - first + 1, has_before if slot < 2 else has_after)
        for slot in (0, 1, NB + 2, NB + 3)
        for first, last in [(max(slot - 4, 0), min(slot, NB - 1))]
    ]
    for slot, at, count, there in outer:
        @pl.when(jnp.logical_not(there))
        def _():
            for k in range(at, at + count):
                rx[slot, k] = jnp.zeros((C, 128), bf16)

    for i in range(NF):
        depths[i] = depth[i:i + 1, :]

    pl.semaphore_wait(barrier, jnp.where(((mine < 2) & has_before) | ((mine > 5) & has_after), 2 * NB, NB))

    def window(ref, i):
        return ref.at[pl.ds(i * W, W)]

    def to_sibling(i):
        return remote(
            window(grad_sib, i), window(sib_rx, i), sib_send.at[i], sib_recv.at[i], sibling, tile
        )

    def start_sibling(s, carry):
        to_sibling((own + s) % NF).start()
        return carry

    lax.fori_loop(1, NF + 1, start_sibling, 0)

    def part_copy(i, at, count):
        return remote(
            out.at[pl.ds(i * W + at, count)], rx.at[mine + 2, pl.ds(at, count)],
            send.at[i], recv.at[mine + 2], 2 * i + core, tile,
        )

    def rim_copy(i, at, count, slot, where):
        return remote(
            out.at[pl.ds(i * W + at, count)], rx.at[slot, pl.ds(at, count)],
            rim_send.at[i], recv.at[slot], 2 * i + core, where,
        )

    def depth_copy(i):
        return remote(
            depths.at[i], depth_rx.at[mine], depth_send.at[i], depth_recv.at[mine], 2 * i + core, tile
        )

    rims = (
        (0, 0, 2, 10, before, has_before), (1, 0, 1, 11, before, has_before),
        (6, 4, 1, 0, after, has_after), (7, 3, 2, 1, after, has_after),
    )

    def add_and_send(s, carry):
        i = (own + s) % NF
        wait_bytes(window(sib_rx, i), sib_recv.at[i])
        for k in range(W):
            out[i * W + k] = (grad_own[i * W + k] + sib_rx[i * W + k].astype(f32)).astype(bf16)
        for b, at, count, slot, where, there in rims:
            @pl.when((mine == b) & there)
            def _():
                rim_copy(i, at, count, slot, where).start()

        @pl.when(i != own)
        def _():
            depth_copy(i).start()
            for least, most, at, count in PARTS:
                @pl.when((mine >= least) & (mine <= most))
                def _():
                    part_copy(i, at, count).start()

        return carry

    lax.fori_loop(1, NF + 1, add_and_send, 0)
    pltpu.make_async_copy(depths.at[own], depth_rx.at[mine], depth_recv.at[mine]).start()
    for least, most, at, count in PARTS:
        @pl.when((mine >= least) & (mine <= most))
        def _():
            pltpu.make_async_copy(
                out.at[pl.ds(own * W + at, count)], rx.at[mine + 2, pl.ds(at, count)], recv.at[mine + 2]
            ).start()

    for b in range(NB):
        wait_bytes(depth_rx.at[b], depth_recv.at[b])
    for slot in range(2, NB + 2):
        first, last = max(slot - 4, 0), min(slot, NB - 1)
        wait_bytes(rx.at[slot, pl.ds(first - slot + 4, last - first + 1)], recv.at[slot])
    for slot, at, count, there in outer:
        @pl.when(there)
        def _():
            wait_bytes(rx.at[slot, pl.ds(at, count)], recv.at[slot])

    def settle(s, carry):
        i = (own + s) % NF
        to_sibling(i).wait_send()
        for b, at, count, slot, where, there in rims:
            @pl.when((mine == b) & there)
            def _():
                rim_copy(i, at, count, slot, where).wait_send()

        @pl.when(i != own)
        def _():
            depth_copy(i).wait_send()
            for least, most, at, count in PARTS:
                @pl.when((mine >= least) & (mine <= most))
                def _():
                    part_copy(i, at, count).wait_send()

        return carry

    lax.fori_loop(1, NF + 1, settle, 0)


def sum_kernel(depth_rx, rx, depth_out, grad_out):
    for b in range(NB):
        depth_out[:, b * 128:(b + 1) * 128] = depth_rx[b]
        total = rx[b, 4].astype(f32)
        for k in range(1, W):
            total += rx[b + k, 4 - k].astype(f32)
        grad_out[:, b * 128:(b + 1) * 128] = total


def per_device(features, views, offsets, kernels, reg_weight, head_weight, depth_cot):
    vmem = pl.BlockSpec(memory_space=pltpu.VMEM)
    smem = pl.BlockSpec(memory_space=pltpu.SMEM)
    hbm = pl.BlockSpec(memory_space=pltpu.HBM)
    dma = pltpu.SemaphoreType.DMA
    shape = jax.ShapeDtypeStruct

    win, index, cot, diag, band, band_t = pl.pallas_call(
        exchange_kernel,
        name="exchange",
        out_shape=(
            shape((ZERO + 1, C, 128), bf16), shape((NF, 128), i32), shape((NF, 128), f32),
            shape((D // 2, 256, 256), bf16), shape((2 * D, D * C), bf16), shape((D * C, 4 * D), bf16),
        ),
        in_specs=[hbm] * 7,
        out_specs=(vmem,) * 6,
        scratch_shapes=[
            pltpu.VMEM((NB, C, 128), bf16),
            pltpu.VMEM((V, NB, D), i32),
            pltpu.VMEM((1, NB * 128), f32),
            pltpu.VMEM((3, 8, C), bf16),
            pltpu.SMEM((V, 16), i32),
            pltpu.SMEM((8,), f32),
            pltpu.VMEM((NB, 1, 256), f32),
            pltpu.VMEM((NF, 1, 256), f32),
            dma((NB,)), dma((NF,)), dma((NB,)), dma((NF,)), dma((4,)), dma((NF,)), dma((NF,)), dma((8,)),
        ],
        compiler_params=pltpu.CompilerParams(
            collective_id=0, has_side_effects=True, vmem_limit_bytes=16 << 20
        ),
    )(
        *(
            pltpu.with_memory_space_constraint(x, pltpu.HBM)
            for x in (
                features.reshape(C, NB * 128), jnp.transpose(offsets[0], (0, 2, 1)), depth_cot, views.T,
                kernels.reshape(D // 2, 2, 128, 128), reg_weight, head_weight,
            )
        )
    )

    depth, grad_own, grad_sib = pl.pallas_call(
        compute_kernel,
        name="compute",
        out_shape=(shape((NF, 128), f32), shape((NF * W, C, 128), f32), shape((NF * W, C, 128), bf16)),
        in_specs=[smem] + [vmem] * 5,
        out_specs=(vmem,) * 3,
        scratch_shapes=[
            pltpu.VMEM((D, NF, V + 1, C, 128), bf16),
            pltpu.VMEM((D * C, NF * 128), bf16),
            pltpu.VMEM((ZERO + 1, C, 128), f32),
            pltpu.VMEM((ZERO + 1, C, 128), f32),
            pltpu.VMEM((NF, C, 128), f32),
        ],
        compiler_params=pltpu.CompilerParams(vmem_limit_bytes=40 << 20),
    )(index, win, diag, band, band_t, cot)

    depth_rx, rx = pl.pallas_call(
        return_kernel,
        name="give_back",
        out_shape=(shape((NB, 1, 128), f32), shape((NB + 4, W, C, 128), bf16)),
        in_specs=[vmem] * 3,
        out_specs=(vmem,) * 2,
        scratch_shapes=[
            pltpu.VMEM((NF * W, C, 128), bf16),
            pltpu.VMEM((NF * W, C, 128), bf16),
            pltpu.VMEM((NF, 1, 128), f32),
            dma((NF,)), dma((NB + 4,)), dma((NF,)), dma((NF,)), dma((NB,)), dma((NF,)), dma((NF,)),
        ],
        compiler_params=pltpu.CompilerParams(
            collective_id=1, has_side_effects=True, vmem_limit_bytes=16 << 20
        ),
    )(grad_own, grad_sib, depth)

    depth_map, grad = pl.pallas_call(
        sum_kernel,
        name="total",
        out_shape=(shape((1, NB * 128), f32), shape((C, NB * 128), f32)),
        in_specs=[vmem] * 2,
        out_specs=(vmem,) * 2,
        compiler_params=pltpu.CompilerParams(vmem_limit_bytes=8 << 20),
    )(depth_rx, rx)
    return depth_map, grad.reshape(1, C, NB * 128)


def solution(mesh):
    return jax.shard_map(
        per_device,
        mesh=mesh,
        in_specs=(
            P("frame", None, "tile"),
            P(),
            P("frame", None, None, "tile"),
            P(),
            P(),
            P(),
            P("frame", "tile"),
        ),
        out_specs=(P("frame", "tile"), P("frame", None, "tile")),
        check_vma=False,
    )
```

```python
import functools

import jax
import jax.numpy as jnp
from jax import lax
from jax.experimental import pallas as pl
from jax.experimental.pallas import tpu as pltpu
from jax.sharding import PartitionSpec as P

MESH = pl.DeviceIdType.MESH
f32, bf16, i32 = jnp.float32, jnp.bfloat16, jnp.int32

C = 32
D = 32
V = 4
NF = 8
NB = 8
W = 5
ZERO = 2 * NF * W

PARTS = ((0, 0, 2, 3), (1, 1, 1, 4), (2, 5, 0, 5), (6, 6, 0, 4), (7, 7, 0, 3))


def place():
    frame = lax.axis_index("frame")
    tile = lax.axis_index("tile")
    core = frame % 2
    own = frame // 2
    return frame, core, own, (own % 4) * 2 + own // 4, tile, lax.axis_size("tile")


def frame_at(block, core):
    return (block % 2) * 8 + (block // 2) * 2 + core


def signal(semaphore, frame, tile):
    pl.semaphore_signal(semaphore, inc=1, device_id=(frame, tile), device_id_type=MESH)


def remote(src, dst, send, recv, frame, tile):
    return pltpu.make_async_remote_copy(
        src_ref=src, dst_ref=dst, send_sem=send, recv_sem=recv, device_id=(frame, tile), device_id_type=MESH
    )


def wait_bytes(ref, semaphore):
    pltpu.make_async_copy(ref, ref, semaphore).wait()


def make_bands(taps, head, band, band_t):
    rows = []
    for t in range(3):
        tap = taps[t].astype(f32)
        rows.append(sum(head[r] * tap[r:r + 1, :] for r in range(8)))
    row_id = lax.broadcasted_iota(i32, (8, C), 0)
    weight = jnp.where(row_id == 0, rows[0], jnp.where(row_id == 1, rows[1], jnp.where(row_id == 2, rows[2], 0.0)))
    w_hi = weight.astype(bf16)
    w_lo = (weight - w_hi.astype(f32)).astype(bf16)
    wide_lane = lax.broadcasted_iota(i32, (C, D * C), 1)
    wide_row = lax.broadcasted_iota(i32, (C, D * C), 0)
    spread = (wide_lane % C == wide_row).astype(f32).astype(bf16)
    tap_of = wide_lane // C - wide_row + 1
    bands = []
    for part in (w_hi, w_lo):
        wide = jnp.dot(part, spread, preferred_element_type=f32)
        bands.append(sum(jnp.where(tap_of == t, wide[t:t + 1, :], 0.0) for t in range(3)))
    band[...] = jnp.concatenate(bands, axis=0).astype(bf16)
    band_t[...] = jnp.transpose(jnp.concatenate(bands + bands, axis=0)).astype(bf16)


def exchange_kernel(
    feats, offsets_hbm, cot_hbm, views_hbm, kernels, taps_hbm, head_hbm,
    win, index_out, cot_out, diag, band, band_t,
    blocks, offsets, cot, taps, views, head, aux, aux_rx,
    send, recv, aux_send, aux_recv, rim_send, sib_send, sib_recv, load,
):
    frame, core, own, mine, tile, tiles = place()
    before, after = (tile + tiles - 1) % tiles, (tile + 1) % tiles
    sibling = frame + 1 - 2 * core

    barrier = pltpu.get_barrier_semaphore()

    def greet(s, carry):
        signal(barrier, frame_at((mine + s) % NB, core), tile)
        return carry

    lax.fori_loop(1, NB, greet, 0)

    has_before, has_after = tile > 0, tile < tiles - 1
    edge = ((mine < 2) & (tile == 0)) | ((mine > 5) & (tile == tiles - 1))

    @pl.when((mine < 2) & has_before)
    def _():
        def greet_before(b, carry):
            signal(barrier, frame_at(b, core), before)
            return carry

        lax.fori_loop(0, NB, greet_before, 0)

    @pl.when((mine > 5) & has_after)
    def _():
        def greet_after(b, carry):
            signal(barrier, frame_at(b, core), after)
            return carry

        lax.fori_loop(0, NB, greet_after, 0)

    signal(barrier, sibling, tile)

    for b in range(NB):
        pltpu.make_async_copy(feats.at[:, pl.ds(b * 128, 128)], blocks.at[b], load.at[0]).start()
    small = [
        pltpu.make_async_copy(src, dst, load.at[n])
        for n, (src, dst) in enumerate(
            ((offsets_hbm, offsets), (cot_hbm, cot), (views_hbm, views), (taps_hbm, taps), (head_hbm, head)), 1
        )
    ]
    half = [
        pltpu.make_async_copy(
            kernels.at[:, h], diag.at[:, pl.ds(h * 128, 128), pl.ds(h * 128, 128)], load.at[6 + h]
        )
        for h in range(2)
    ]
    for copy in small:
        copy.start()
    for copy in half:
        copy.start()
    win[ZERO] = jnp.zeros((C, 128), bf16)
    for b, outside in ((0, (0, 1)), (1, (0,)), (6, (4,)), (7, (3, 4))):
        @pl.when((mine == b) & edge)
        def _():
            for i in range(NF):
                for k in outside:
                    win[i * W + k] = jnp.zeros((C, 128), bf16)

    small[0].wait()
    small[1].wait()
    for b in range(NB):
        for j in range(V):
            aux[b, :, j * D:(j + 1) * D] = offsets[j, b:b + 1, :].astype(f32)
        aux[b, :, 128:256] = cot[:, b * 128:(b + 1) * 128]
    wait_bytes(blocks, load.at[0])

    pl.semaphore_wait(barrier, NB + jnp.where(has_before, 2, 0) + jnp.where(has_after, 2, 0))

    rims = (
        (0, 1, 4, 6, before, has_before), (0, 2, 3, 7, before, has_before),
        (6, 2, 0, 0, after, has_after), (7, 1, 0, 1, after, has_after),
    )
    rim_copies = [
        (
            remote(
                blocks.at[pl.ds(first, count)], win.at[pl.ds(own * W + at, count)],
                rim_send.at[n], recv.at[own], frame_at(b, core), where,
            ),
            there,
        )
        for n, (first, count, at, b, where, there) in enumerate(rims)
    ]
    for copy, there in rim_copies:
        @pl.when(there)
        def _():
            copy.start()

    def part_copy(b, at, count):
        return remote(
            blocks.at[pl.ds(b - 2 + at, count)], win.at[pl.ds(own * W + at, count)],
            send.at[b], recv.at[own], frame_at(b, core), tile,
        )

    def aux_copy(b):
        return remote(aux.at[b], aux_rx.at[own], aux_send.at[b], aux_recv.at[own], frame_at(b, core), tile)

    def start(s, carry):
        b = (mine + s) % NB
        aux_copy(b).start()
        for least, most, at, count in PARTS:
            @pl.when((b >= least) & (b <= most))
            def _():
                part_copy(b, at, count).start()
        return carry

    lax.fori_loop(1, NB, start, 0)
    pltpu.make_async_copy(aux.at[mine], aux_rx.at[own], aux_recv.at[own]).start()
    for least, most, at, count in PARTS:
        @pl.when((mine >= least) & (mine <= most))
        def _():
            pltpu.make_async_copy(
                blocks.at[pl.ds(mine - 2 + at, count)], win.at[pl.ds(own * W + at, count)], recv.at[own]
            ).start()

    corner = jnp.zeros((D // 2, 128, 128), bf16)
    diag[:, 0:128, 128:256] = corner
    diag[:, 128:256, 0:128] = corner

    def window(i):
        return win.at[pl.ds(i * W, W)]

    def to_sibling(i):
        return remote(
            window(i), window(NF + i), sib_send.at[i], sib_recv.at[i], sibling, tile
        )

    def forward(s, carry):
        i = (own + s) % NF
        @pl.when(jnp.logical_not(edge))
        def _():
            wait_bytes(window(i), recv.at[i])

        for b, _, at, count in PARTS:
            if count < W:
                @pl.when((mine == b) & edge)
                def _():
                    wait_bytes(win.at[pl.ds(i * W + at, count)], recv.at[i])
        to_sibling(i).start()
        return carry

    lax.fori_loop(0, NF, forward, 0)

    for copy in small[2:]:
        copy.wait()
    make_bands(taps, head, band, band_t)

    view_of = lax.broadcasted_iota(i32, (1, 128), 1) // D
    here = tile * NB + mine
    for i in range(NF):
        wait_bytes(aux_rx.at[i], aux_recv.at[i])
        shift = aux_rx[i, :, 0:128].astype(i32)
        at = here + shift
        row = jnp.zeros((1, 128), i32)
        for j in range(V):
            v = views[j, 2 * i + core]
            row = jnp.where(view_of == j, jnp.where(v % 2 == core, 0, NF * W) + (v // 2) * W + 2, row)
        index_out[i:i + 1, :] = jnp.where((at >= 0) & (at < tiles * NB), row + shift, ZERO)
        cot_out[i:i + 1, :] = aux_rx[i, :, 128:256]

    def settle(s, carry):
        b = (mine + s) % NB
        aux_copy(b).wait_send()
        for least, most, at, count in PARTS:
            @pl.when((b >= least) & (b <= most))
            def _():
                part_copy(b, at, count).wait_send()
        return carry

    lax.fori_loop(1, NB, settle, 0)
    for copy, there in rim_copies:
        @pl.when(there)
        def _():
            copy.wait_send()

    def settle_sibling(i, carry):
        to_sibling(i).wait_send()
        wait_bytes(window(NF + i), sib_recv.at[i])
        return carry

    lax.fori_loop(0, NF, settle_sibling, 0)
    for copy in half:
        copy.wait()


def compute_kernel(idx, win, diag, band, band_t, cot, depth_out, acc, ref_acc, cen, vd):
    step = 2
    mean_of = 1.0 / (V + 1)

    for p in range(D // 2):
        mat = diag[p]
        for i0 in range(0, NF, step):
            picks = [
                jnp.concatenate([win[idx[i, j * D + 2 * p + h]] for h in range(2)], axis=1)
                for i in range(i0, i0 + step) for j in range(V)
            ]
            y = jnp.dot(jnp.concatenate(picks, axis=0), mat, preferred_element_type=f32)
            for i in range(i0, i0 + step):
                for h in range(2):
                    o, d = (i - i0) * V * C, 2 * p + h
                    xs = [win[i * W + 2].astype(f32)]
                    xs += [y[o + j * C:o + (j + 1) * C, h * 128:(h + 1) * 128] for j in range(V)]
                    average = (((xs[0] + xs[1]) + (xs[2] + xs[3])) + xs[4]) * mean_of
                    cs = [x - average for x in xs]
                    sq = [c * c for c in cs]
                    variance = (((sq[0] + sq[1]) + (sq[2] + sq[3])) + sq[4]) * mean_of
                    vd[d * C:(d + 1) * C, i * 128:(i + 1) * 128] = variance.astype(bf16)
                    for j in range(V + 1):
                        cen[d, i, j] = cs[j].astype(bf16)

    value = (lax.broadcasted_iota(i32, (D, 128), 0).astype(f32) + 1.0) / D
    for i0 in range(0, NF, 2):
        both = jnp.dot(band[...], vd[:, i0 * 128:(i0 + 2) * 128], preferred_element_type=f32)
        parts = []
        for i in range(i0, i0 + 2):
            o = (i - i0) * 128
            th = jnp.tanh(both[:D, o:o + 128] + both[D:, o:o + 128])
            w = jnp.exp(4.0 * th)
            total = jnp.sum(w, axis=0, keepdims=True)
            depth = jnp.sum(w * value, axis=0, keepdims=True) / total
            depth_out[i] = depth
            scale = cot[i:i + 1, :] / total * (4.0 * 2.0 / (V + 1))
            d_pre = (w * (value - depth)) * scale * (1.0 - th * th)
            hi = d_pre.astype(bf16)
            lo = (d_pre - hi.astype(f32)).astype(bf16)
            parts.append(jnp.concatenate([hi, hi, lo, lo], axis=0))
        rhs = jnp.concatenate(parts, axis=1)
        vd[:, i0 * 128:(i0 + 2) * 128] = jnp.dot(band_t[...], rhs, preferred_element_type=f32).astype(bf16)

    acc[...] = jnp.zeros_like(acc)
    ref_acc[...] = jnp.zeros_like(ref_acc)

    for p in range(D // 2):
        mat = diag[p]
        for i0 in range(0, NF, step):
            gs = []
            for i in range(i0, i0 + step):
                dvs = [vd[(2 * p + h) * C:(2 * p + h + 1) * C, i * 128:(i + 1) * 128] for h in range(2)]
                ref_acc[i] += (dvs[0] * cen[2 * p, i, 0]).astype(f32) + (dvs[1] * cen[2 * p + 1, i, 0]).astype(f32)
                for j in range(V):
                    gs.append(jnp.concatenate([dvs[h] * cen[2 * p + h, i, j + 1] for h in range(2)], axis=1))
            y = lax.dot_general(
                jnp.concatenate(gs, axis=0), mat, (((1,), (1,)), ((), ())), preferred_element_type=f32
            )
            for h in range(2):
                for i in range(i0, i0 + step):
                    slots = [idx[i, j * D + 2 * p + h] for j in range(V)]
                    o = (i - i0) * V * C
                    new = [acc[slots[j]] + y[o + j * C:o + (j + 1) * C, h * 128:(h + 1) * 128] for j in range(V)]
                    for j in range(V):
                        acc[slots[j]] = new[j]


def return_kernel(
    acc, ref_acc, depths, depth_rx, rx,
    grad_sib, sib_rx, out, send, recv, rim_send, depth_send, depth_recv, sib_send, sib_recv,
):
    frame, core, own, mine, tile, tiles = place()
    before, after = (tile + tiles - 1) % tiles, (tile + 1) % tiles
    sibling = frame + 1 - 2 * core

    barrier = pltpu.get_barrier_semaphore()
    signal(barrier, sibling, tile)

    def greet(s, carry):
        signal(barrier, frame_at((mine + s) % NB, core), tile)
        return carry

    lax.fori_loop(1, NB, greet, 0)
    has_before, has_after = tile > 0, tile < tiles - 1

    @pl.when(has_before)
    def _():
        for b in (6, 7):
            signal(barrier, frame_at(b, core), before)

    @pl.when(has_after)
    def _():
        for b in (0, 1):
            signal(barrier, frame_at(b, core), after)

    outer = [
        (slot, first - slot + 4, last - first + 1, has_before if slot < 2 else has_after)
        for slot in (0, 1, NB + 2, NB + 3)
        for first, last in [(max(slot - 4, 0), min(slot, NB - 1))]
    ]
    for slot, at, count, there in outer:
        @pl.when(jnp.logical_not(there))
        def _():
            for k in range(at, at + count):
                rx[slot, k] = jnp.zeros((C, 128), bf16)

    for s in range(NF * W):
        grad_sib[s] = acc[NF * W + s].astype(bf16)

    pl.semaphore_wait(barrier, jnp.where(((mine < 2) & has_before) | ((mine > 5) & has_after), 2 * NB, NB))

    def window(ref, i):
        return ref.at[pl.ds(i * W, W)]

    def to_sibling(i):
        return remote(
            window(grad_sib, i), window(sib_rx, i), sib_send.at[i], sib_recv.at[i], sibling, tile
        )

    def start_sibling(s, carry):
        to_sibling((own + s) % NF).start()
        return carry

    lax.fori_loop(1, NF + 1, start_sibling, 0)

    def part_copy(i, at, count):
        return remote(
            out.at[pl.ds(i * W + at, count)], rx.at[mine + 2, pl.ds(at, count)],
            send.at[i], recv.at[mine + 2], 2 * i + core, tile,
        )

    def rim_copy(i, at, count, slot, where):
        return remote(
            out.at[pl.ds(i * W + at, count)], rx.at[slot, pl.ds(at, count)],
            rim_send.at[i], recv.at[slot], 2 * i + core, where,
        )

    def depth_copy(i):
        return remote(
            depths.at[i], depth_rx.at[mine], depth_send.at[i], depth_recv.at[mine], 2 * i + core, tile
        )

    rims = (
        (0, 0, 2, 10, before, has_before), (1, 0, 1, 11, before, has_before),
        (6, 4, 1, 0, after, has_after), (7, 3, 2, 1, after, has_after),
    )

    def add_and_send(s, carry):
        i = (own + s) % NF
        wait_bytes(window(sib_rx, i), sib_recv.at[i])
        for k in range(W):
            total = acc[i * W + k] + sib_rx[i * W + k].astype(f32)
            out[i * W + k] = (total + ref_acc[i] if k == 2 else total).astype(bf16)
        for b, at, count, slot, where, there in rims:
            @pl.when((mine == b) & there)
            def _():
                rim_copy(i, at, count, slot, where).start()

        @pl.when(i != own)
        def _():
            depth_copy(i).start()
            for least, most, at, count in PARTS:
                @pl.when((mine >= least) & (mine <= most))
                def _():
                    part_copy(i, at, count).start()

        return carry

    lax.fori_loop(1, NF + 1, add_and_send, 0)
    pltpu.make_async_copy(depths.at[own], depth_rx.at[mine], depth_recv.at[mine]).start()
    for least, most, at, count in PARTS:
        @pl.when((mine >= least) & (mine <= most))
        def _():
            pltpu.make_async_copy(
                out.at[pl.ds(own * W + at, count)], rx.at[mine + 2, pl.ds(at, count)], recv.at[mine + 2]
            ).start()

    for b in range(NB):
        wait_bytes(depth_rx.at[b], depth_recv.at[b])
    for slot in range(2, NB + 2):
        first, last = max(slot - 4, 0), min(slot, NB - 1)
        wait_bytes(rx.at[slot, pl.ds(first - slot + 4, last - first + 1)], recv.at[slot])
    for slot, at, count, there in outer:
        @pl.when(there)
        def _():
            wait_bytes(rx.at[slot, pl.ds(at, count)], recv.at[slot])

    def settle(s, carry):
        i = (own + s) % NF
        to_sibling(i).wait_send()
        for b, at, count, slot, where, there in rims:
            @pl.when((mine == b) & there)
            def _():
                rim_copy(i, at, count, slot, where).wait_send()

        @pl.when(i != own)
        def _():
            depth_copy(i).wait_send()
            for least, most, at, count in PARTS:
                @pl.when((mine >= least) & (mine <= most))
                def _():
                    part_copy(i, at, count).wait_send()

        return carry

    lax.fori_loop(1, NF + 1, settle, 0)


def sum_kernel(depth_rx, rx, depth_out, grad_out):
    for b in range(NB):
        depth_out[:, b * 128:(b + 1) * 128] = depth_rx[b]
        total = rx[b, 4].astype(f32)
        for k in range(1, W):
            total += rx[b + k, 4 - k].astype(f32)
        grad_out[:, b * 128:(b + 1) * 128] = total


def per_device(features, views, offsets, kernels, reg_weight, head_weight, depth_cot):
    vmem = pl.BlockSpec(memory_space=pltpu.VMEM)
    smem = pl.BlockSpec(memory_space=pltpu.SMEM)
    hbm = pl.BlockSpec(memory_space=pltpu.HBM)
    dma = pltpu.SemaphoreType.DMA
    shape = jax.ShapeDtypeStruct

    win, index, cot, diag, band, band_t = pl.pallas_call(
        exchange_kernel,
        name="exchange",
        out_shape=(
            shape((ZERO + 1, C, 128), bf16), shape((NF, 128), i32), shape((NF, 128), f32),
            shape((D // 2, 256, 256), bf16), shape((2 * D, D * C), bf16), shape((D * C, 4 * D), bf16),
        ),
        in_specs=[hbm] * 7,
        out_specs=(vmem,) * 6,
        scratch_shapes=[
            pltpu.VMEM((NB, C, 128), bf16),
            pltpu.VMEM((V, NB, D), i32),
            pltpu.VMEM((1, NB * 128), f32),
            pltpu.VMEM((3, 8, C), bf16),
            pltpu.SMEM((V, 16), i32),
            pltpu.SMEM((8,), f32),
            pltpu.VMEM((NB, 1, 256), f32),
            pltpu.VMEM((NF, 1, 256), f32),
            dma((NB,)), dma((NF,)), dma((NB,)), dma((NF,)), dma((4,)), dma((NF,)), dma((NF,)), dma((8,)),
        ],
        compiler_params=pltpu.CompilerParams(
            collective_id=0, has_side_effects=True, vmem_limit_bytes=16 << 20
        ),
    )(
        *(
            pltpu.with_memory_space_constraint(x, pltpu.HBM)
            for x in (
                features.reshape(C, NB * 128), jnp.transpose(offsets[0], (0, 2, 1)), depth_cot, views.T,
                kernels.reshape(D // 2, 2, 128, 128), reg_weight, head_weight,
            )
        )
    )

    depths, acc, ref_acc = pl.pallas_call(
        compute_kernel,
        name="compute",
        out_shape=(shape((NF, 1, 128), f32), shape((ZERO + 1, C, 128), f32), shape((NF, C, 128), f32)),
        in_specs=[smem] + [vmem] * 5,
        out_specs=(vmem,) * 3,
        scratch_shapes=[
            pltpu.VMEM((D, NF, V + 1, C, 128), bf16),
            pltpu.VMEM((D * C, NF * 128), bf16),
        ],
        compiler_params=pltpu.CompilerParams(vmem_limit_bytes=40 << 20),
    )(index, win, diag, band, band_t, cot)

    depth_rx, rx = pl.pallas_call(
        return_kernel,
        name="give_back",
        out_shape=(shape((NB, 1, 128), f32), shape((NB + 4, W, C, 128), bf16)),
        in_specs=[vmem] * 3,
        out_specs=(vmem,) * 2,
        scratch_shapes=[
            pltpu.VMEM((NF * W, C, 128), bf16),
            pltpu.VMEM((NF * W, C, 128), bf16),
            pltpu.VMEM((NF * W, C, 128), bf16),
            dma((NF,)), dma((NB + 4,)), dma((NF,)), dma((NF,)), dma((NB,)), dma((NF,)), dma((NF,)),
        ],
        compiler_params=pltpu.CompilerParams(
            collective_id=1, has_side_effects=True, vmem_limit_bytes=16 << 20
        ),
    )(acc, ref_acc, depths)

    depth_map, grad = pl.pallas_call(
        sum_kernel,
        name="total",
        out_shape=(shape((1, NB * 128), f32), shape((C, NB * 128), f32)),
        in_specs=[vmem] * 2,
        out_specs=(vmem,) * 2,
        compiler_params=pltpu.CompilerParams(vmem_limit_bytes=8 << 20),
    )(depth_rx, rx)
    return depth_map, grad.reshape(1, C, NB * 128)


def solution(mesh):
    return jax.shard_map(
        per_device,
        mesh=mesh,
        in_specs=(
            P("frame", None, "tile"),
            P(),
            P("frame", None, None, "tile"),
            P(),
            P(),
            P(),
            P("frame", "tile"),
        ),
        out_specs=(P("frame", "tile"), P("frame", None, "tile")),
        check_vma=False,
    )
```

```python
import functools

import jax
import jax.numpy as jnp
from jax import lax
from jax.experimental import pallas as pl
from jax.experimental.pallas import tpu as pltpu
from jax.sharding import PartitionSpec as P

MESH = pl.DeviceIdType.MESH
f32, bf16, i32 = jnp.float32, jnp.bfloat16, jnp.int32

C = 32
D = 32
V = 4
NF = 8
NB = 8
W = 5
ZERO = 2 * NF * W

PARTS = ((0, 0, 2, 3), (1, 1, 1, 4), (2, 5, 0, 5), (6, 6, 0, 4), (7, 7, 0, 3))


def place():
    frame = lax.axis_index("frame")
    tile = lax.axis_index("tile")
    core = frame % 2
    own = frame // 2
    return frame, core, own, (own % 4) * 2 + own // 4, tile, lax.axis_size("tile")


def frame_at(block, core):
    return (block % 2) * 8 + (block // 2) * 2 + core


def signal(semaphore, frame, tile):
    pl.semaphore_signal(semaphore, inc=1, device_id=(frame, tile), device_id_type=MESH)


def remote(src, dst, send, recv, frame, tile):
    return pltpu.make_async_remote_copy(
        src_ref=src, dst_ref=dst, send_sem=send, recv_sem=recv, device_id=(frame, tile), device_id_type=MESH
    )


def wait_bytes(ref, semaphore):
    pltpu.make_async_copy(ref, ref, semaphore).wait()


def make_bands(taps, head, band, columns):
    rows = []
    for t in range(3):
        tap = taps[t].astype(f32)
        rows.append(sum(head[r] * tap[r:r + 1, :] for r in range(8)))
    row_id = lax.broadcasted_iota(i32, (8, C), 0)
    weight = jnp.where(row_id == 0, rows[0], jnp.where(row_id == 1, rows[1], jnp.where(row_id == 2, rows[2], 0.0)))
    w_hi = weight.astype(bf16)
    w_lo = (weight - w_hi.astype(f32)).astype(bf16)
    wide_lane = lax.broadcasted_iota(i32, (C, D * C), 1)
    wide_row = lax.broadcasted_iota(i32, (C, D * C), 0)
    spread = (wide_lane % C == wide_row).astype(f32).astype(bf16)
    tap_of = wide_lane // C - wide_row + 1
    bands = []
    for part in (w_hi, w_lo):
        wide = jnp.dot(part, spread, preferred_element_type=f32)
        bands.append(sum(jnp.where(tap_of == t, wide[t:t + 1, :], 0.0) for t in range(3)))
    band[...] = jnp.concatenate(bands, axis=0).astype(bf16)
    upright = jnp.transpose(jnp.concatenate([weight, jnp.zeros((8, 128 - C), f32)], axis=1))
    for t in range(3):
        columns[t] = jnp.broadcast_to(upright[:C, t:t + 1], (C, 128))


def exchange_kernel(
    feats, offsets_hbm, cot_hbm, views_hbm, kernels, taps_hbm, head_hbm,
    win, index_out, cot_out, diag, band, columns,
    blocks, offsets, cot, taps, views, head, aux, aux_rx,
    send, recv, aux_send, aux_recv, rim_send, sib_send, sib_recv, load,
):
    frame, core, own, mine, tile, tiles = place()
    before, after = (tile + tiles - 1) % tiles, (tile + 1) % tiles
    sibling = frame + 1 - 2 * core

    barrier = pltpu.get_barrier_semaphore()

    def greet(s, carry):
        signal(barrier, frame_at((mine + s) % NB, core), tile)
        return carry

    lax.fori_loop(1, NB, greet, 0)

    has_before, has_after = tile > 0, tile < tiles - 1
    edge = ((mine < 2) & (tile == 0)) | ((mine > 5) & (tile == tiles - 1))

    @pl.when((mine < 2) & has_before)
    def _():
        def greet_before(b, carry):
            signal(barrier, frame_at(b, core), before)
            return carry

        lax.fori_loop(0, NB, greet_before, 0)

    @pl.when((mine > 5) & has_after)
    def _():
        def greet_after(b, carry):
            signal(barrier, frame_at(b, core), after)
            return carry

        lax.fori_loop(0, NB, greet_after, 0)

    signal(barrier, sibling, tile)

    for b in range(NB):
        pltpu.make_async_copy(feats.at[:, pl.ds(b * 128, 128)], blocks.at[b], load.at[0]).start()
    small = [
        pltpu.make_async_copy(src, dst, load.at[n])
        for n, (src, dst) in enumerate(
            ((offsets_hbm, offsets), (cot_hbm, cot), (views_hbm, views), (taps_hbm, taps), (head_hbm, head)), 1
        )
    ]
    half = [
        pltpu.make_async_copy(
            kernels.at[:, h], diag.at[:, pl.ds(h * 128, 128), pl.ds(h * 128, 128)], load.at[6 + h]
        )
        for h in range(2)
    ]
    for copy in small:
        copy.start()
    for copy in half:
        copy.start()
    win[ZERO] = jnp.zeros((C, 128), bf16)
    for b, outside in ((0, (0, 1)), (1, (0,)), (6, (4,)), (7, (3, 4))):
        @pl.when((mine == b) & edge)
        def _():
            for i in range(NF):
                for k in outside:
                    win[i * W + k] = jnp.zeros((C, 128), bf16)

    small[0].wait()
    small[1].wait()
    for b in range(NB):
        for j in range(V):
            aux[b, :, j * D:(j + 1) * D] = offsets[j, b:b + 1, :].astype(f32)
        aux[b, :, 128:256] = cot[:, b * 128:(b + 1) * 128]
    wait_bytes(blocks, load.at[0])

    pl.semaphore_wait(barrier, NB + jnp.where(has_before, 2, 0) + jnp.where(has_after, 2, 0))

    rims = (
        (0, 1, 4, 6, before, has_before), (0, 2, 3, 7, before, has_before),
        (6, 2, 0, 0, after, has_after), (7, 1, 0, 1, after, has_after),
    )
    rim_copies = [
        (
            remote(
                blocks.at[pl.ds(first, count)], win.at[pl.ds(own * W + at, count)],
                rim_send.at[n], recv.at[own], frame_at(b, core), where,
            ),
            there,
        )
        for n, (first, count, at, b, where, there) in enumerate(rims)
    ]
    for copy, there in rim_copies:
        @pl.when(there)
        def _():
            copy.start()

    def part_copy(b, at, count):
        return remote(
            blocks.at[pl.ds(b - 2 + at, count)], win.at[pl.ds(own * W + at, count)],
            send.at[b], recv.at[own], frame_at(b, core), tile,
        )

    def aux_copy(b):
        return remote(aux.at[b], aux_rx.at[own], aux_send.at[b], aux_recv.at[own], frame_at(b, core), tile)

    def start(n, carry):
        b = (mine + jnp.where(n % 2 == 1, 4 - (n + 1) // 2, 4 + n // 2)) % NB
        aux_copy(b).start()
        for least, most, at, count in PARTS:
            @pl.when((b >= least) & (b <= most))
            def _():
                part_copy(b, at, count).start()
        return carry

    lax.fori_loop(0, NB - 1, start, 0)
    pltpu.make_async_copy(aux.at[mine], aux_rx.at[own], aux_recv.at[own]).start()
    for least, most, at, count in PARTS:
        @pl.when((mine >= least) & (mine <= most))
        def _():
            pltpu.make_async_copy(
                blocks.at[pl.ds(mine - 2 + at, count)], win.at[pl.ds(own * W + at, count)], recv.at[own]
            ).start()

    corner = jnp.zeros((D // 2, 128, 128), bf16)
    diag[:, 0:128, 128:256] = corner
    diag[:, 128:256, 0:128] = corner
    for copy in small[2:]:
        copy.wait()
    make_bands(taps, head, band, columns)

    def window(i):
        return win.at[pl.ds(i * W, W)]

    def to_sibling(i):
        return remote(
            window(i), window(NF + i), sib_send.at[i], sib_recv.at[i], sibling, tile
        )

    def forward(s, carry):
        i = (own + s) % NF
        @pl.when(jnp.logical_not(edge))
        def _():
            wait_bytes(window(i), recv.at[i])

        for b, _, at, count in PARTS:
            if count < W:
                @pl.when((mine == b) & edge)
                def _():
                    wait_bytes(win.at[pl.ds(i * W + at, count)], recv.at[i])
        to_sibling(i).start()
        return carry

    lax.fori_loop(0, NF, forward, 0)

    view_of = lax.broadcasted_iota(i32, (1, 128), 1) // D
    here = tile * NB + mine
    for i in range(NF):
        wait_bytes(aux_rx.at[i], aux_recv.at[i])
        shift = aux_rx[i, :, 0:128].astype(i32)
        at = here + shift
        row = jnp.zeros((1, 128), i32)
        for j in range(V):
            v = views[j, 2 * i + core]
            row = jnp.where(view_of == j, jnp.where(v % 2 == core, 0, NF * W) + (v // 2) * W + 2, row)
        index_out[i:i + 1, :] = jnp.where((at >= 0) & (at < tiles * NB), row + shift, ZERO)
        cot_out[i:i + 1, :] = aux_rx[i, :, 128:256]

    def settle(s, carry):
        b = (mine + s) % NB
        aux_copy(b).wait_send()
        for least, most, at, count in PARTS:
            @pl.when((b >= least) & (b <= most))
            def _():
                part_copy(b, at, count).wait_send()
        return carry

    lax.fori_loop(1, NB, settle, 0)
    for copy, there in rim_copies:
        @pl.when(there)
        def _():
            copy.wait_send()

    def settle_sibling(i, carry):
        to_sibling(i).wait_send()
        wait_bytes(window(NF + i), sib_recv.at[i])
        return carry

    lax.fori_loop(0, NF, settle_sibling, 0)
    for copy in half:
        copy.wait()


def compute_kernel(idx, win, diag, band, columns, cot, depth_out, acc, ref_acc, cen, vd, d_pre):
    step = 2
    mean_of = 1.0 / (V + 1)

    for p in range(D // 2):
        mat = diag[p]
        for i0 in range(0, NF, step):
            picks = [
                jnp.concatenate([win[idx[i, j * D + 2 * p + h]] for h in range(2)], axis=1)
                for i in range(i0, i0 + step) for j in range(V)
            ]
            y = jnp.dot(jnp.concatenate(picks, axis=0), mat, preferred_element_type=f32)
            for i in range(i0, i0 + step):
                for h in range(2):
                    o, d = (i - i0) * V * C, 2 * p + h
                    xs = [win[i * W + 2].astype(f32)]
                    xs += [y[o + j * C:o + (j + 1) * C, h * 128:(h + 1) * 128] for j in range(V)]
                    average = (((xs[0] + xs[1]) + (xs[2] + xs[3])) + xs[4]) * mean_of
                    cs = [x - average for x in xs]
                    sq = [c * c for c in cs]
                    variance = (((sq[0] + sq[1]) + (sq[2] + sq[3])) + sq[4]) * mean_of
                    vd[d * C:(d + 1) * C, i * 128:(i + 1) * 128] = variance.astype(bf16)
                    for j in range(V + 1):
                        cen[d, i, j] = cs[j].astype(bf16)

    value = (lax.broadcasted_iota(i32, (D, 128), 0).astype(f32) + 1.0) / D
    for i0 in range(0, NF, 2):
        both = jnp.dot(band[...], vd[:, i0 * 128:(i0 + 2) * 128], preferred_element_type=f32)
        for i in range(i0, i0 + 2):
            o = (i - i0) * 128
            th = jnp.tanh(both[:D, o:o + 128] + both[D:, o:o + 128])
            w = jnp.exp(4.0 * th)
            total = jnp.sum(w, axis=0, keepdims=True)
            depth = jnp.sum(w * value, axis=0, keepdims=True) / total
            depth_out[i] = depth
            scale = cot[i:i + 1, :] / total * (4.0 * 2.0 / (V + 1))
            d_pre[i] = (w * (value - depth)) * scale * (1.0 - th * th)

    acc[...] = jnp.zeros_like(acc)
    ref_acc[...] = jnp.zeros_like(ref_acc)

    for p in range(D // 2):
        mat = diag[p]
        for i0 in range(0, NF, step):
            gs = []
            for i in range(i0, i0 + step):
                dvs = []
                for d in (2 * p, 2 * p + 1):
                    terms = [columns[t] * d_pre[i, d - t + 1:d - t + 2, :] for t in range(3) if 0 <= d - t + 1 < D]
                    dvs.append(sum(terms[1:], terms[0]).astype(bf16))
                ref_acc[i] += (dvs[0] * cen[2 * p, i, 0]).astype(f32) + (dvs[1] * cen[2 * p + 1, i, 0]).astype(f32)
                for j in range(V):
                    gs.append(jnp.concatenate([dvs[h] * cen[2 * p + h, i, j + 1] for h in range(2)], axis=1))
            y = lax.dot_general(
                jnp.concatenate(gs, axis=0), mat, (((1,), (1,)), ((), ())), preferred_element_type=f32
            )
            for h in range(2):
                for i in range(i0, i0 + step):
                    slots = [idx[i, j * D + 2 * p + h] for j in range(V)]
                    o = (i - i0) * V * C
                    new = [acc[slots[j]] + y[o + j * C:o + (j + 1) * C, h * 128:(h + 1) * 128] for j in range(V)]
                    for j in range(V):
                        acc[slots[j]] = new[j]


def return_kernel(
    acc, ref_acc, depths, depth_rx, rx,
    grad_sib, sib_rx, out, send, recv, rim_send, depth_send, depth_recv, sib_send, sib_recv,
):
    frame, core, own, mine, tile, tiles = place()
    before, after = (tile + tiles - 1) % tiles, (tile + 1) % tiles
    sibling = frame + 1 - 2 * core

    barrier = pltpu.get_barrier_semaphore()
    signal(barrier, sibling, tile)

    def greet(s, carry):
        signal(barrier, frame_at((mine + s) % NB, core), tile)
        return carry

    lax.fori_loop(1, NB, greet, 0)
    has_before, has_after = tile > 0, tile < tiles - 1

    @pl.when(has_before)
    def _():
        for b in (6, 7):
            signal(barrier, frame_at(b, core), before)

    @pl.when(has_after)
    def _():
        for b in (0, 1):
            signal(barrier, frame_at(b, core), after)

    outer = [
        (slot, first - slot + 4, last - first + 1, has_before if slot < 2 else has_after)
        for slot in (0, 1, NB + 2, NB + 3)
        for first, last in [(max(slot - 4, 0), min(slot, NB - 1))]
    ]
    for slot, at, count, there in outer:
        @pl.when(jnp.logical_not(there))
        def _():
            for k in range(at, at + count):
                rx[slot, k] = jnp.zeros((C, 128), bf16)

    for s in range(NF * W):
        grad_sib[s] = acc[NF * W + s].astype(bf16)

    pl.semaphore_wait(barrier, jnp.where(((mine < 2) & has_before) | ((mine > 5) & has_after), 2 * NB, NB))

    def window(ref, i):
        return ref.at[pl.ds(i * W, W)]

    def to_sibling(i):
        return remote(
            window(grad_sib, i), window(sib_rx, i), sib_send.at[i], sib_recv.at[i], sibling, tile
        )

    def owner(n):
        across, along = 1 - n % 2, jnp.where(n < 2, 2, jnp.where(n < 4, 1, jnp.where(n < 6, 3, 0)))
        return ((own // 4 + across) % 2) * 4 + (own % 4 + along) % 4

    def start_sibling(n, carry):
        to_sibling(owner(n)).start()
        return carry

    lax.fori_loop(0, NF, start_sibling, 0)

    def part_copy(i, at, count):
        return remote(
            out.at[pl.ds(i * W + at, count)], rx.at[mine + 2, pl.ds(at, count)],
            send.at[i], recv.at[mine + 2], 2 * i + core, tile,
        )

    def rim_copy(i, at, count, slot, where):
        return remote(
            out.at[pl.ds(i * W + at, count)], rx.at[slot, pl.ds(at, count)],
            rim_send.at[i], recv.at[slot], 2 * i + core, where,
        )

    def depth_copy(i):
        return remote(
            depths.at[i], depth_rx.at[mine], depth_send.at[i], depth_recv.at[mine], 2 * i + core, tile
        )

    rims = (
        (0, 0, 2, 10, before, has_before), (1, 0, 1, 11, before, has_before),
        (6, 4, 1, 0, after, has_after), (7, 3, 2, 1, after, has_after),
    )

    def send_parts(i):
        @pl.when(i != own)
        def _():
            depth_copy(i).start()
            for least, most, at, count in PARTS:
                @pl.when((mine >= least) & (mine <= most))
                def _():
                    part_copy(i, at, count).start()

    at_edge = (mine < 2) | (mine > 5)

    def add_and_send(n, carry):
        i = owner(n)
        wait_bytes(window(sib_rx, i), sib_recv.at[i])
        for k in range(W):
            total = acc[i * W + k] + sib_rx[i * W + k].astype(f32)
            out[i * W + k] = (total + ref_acc[i] if k == 2 else total).astype(bf16)
        for b, at, count, slot, where, there in rims:
            @pl.when((mine == b) & there)
            def _():
                rim_copy(i, at, count, slot, where).start()

        @pl.when(jnp.logical_not(at_edge))
        def _():
            send_parts(i)

        return carry

    lax.fori_loop(0, NF, add_and_send, 0)

    @pl.when(at_edge)
    def _():
        def send_later(n, carry):
            send_parts(owner(n))
            return carry

        lax.fori_loop(0, NF, send_later, 0)

    pltpu.make_async_copy(depths.at[own], depth_rx.at[mine], depth_recv.at[mine]).start()
    for least, most, at, count in PARTS:
        @pl.when((mine >= least) & (mine <= most))
        def _():
            pltpu.make_async_copy(
                out.at[pl.ds(own * W + at, count)], rx.at[mine + 2, pl.ds(at, count)], recv.at[mine + 2]
            ).start()

    for b in range(NB):
        wait_bytes(depth_rx.at[b], depth_recv.at[b])
    for slot in range(2, NB + 2):
        first, last = max(slot - 4, 0), min(slot, NB - 1)
        wait_bytes(rx.at[slot, pl.ds(first - slot + 4, last - first + 1)], recv.at[slot])
    for slot, at, count, there in outer:
        @pl.when(there)
        def _():
            wait_bytes(rx.at[slot, pl.ds(at, count)], recv.at[slot])

    def settle(s, carry):
        i = (own + s) % NF
        to_sibling(i).wait_send()
        for b, at, count, slot, where, there in rims:
            @pl.when((mine == b) & there)
            def _():
                rim_copy(i, at, count, slot, where).wait_send()

        @pl.when(i != own)
        def _():
            depth_copy(i).wait_send()
            for least, most, at, count in PARTS:
                @pl.when((mine >= least) & (mine <= most))
                def _():
                    part_copy(i, at, count).wait_send()

        return carry

    lax.fori_loop(1, NF + 1, settle, 0)


def sum_kernel(depth_rx, rx, depth_out, grad_out):
    for b in range(NB):
        depth_out[:, b * 128:(b + 1) * 128] = depth_rx[b]
        total = rx[b, 4].astype(f32)
        for k in range(1, W):
            total += rx[b + k, 4 - k].astype(f32)
        grad_out[:, b * 128:(b + 1) * 128] = total


def per_device(features, views, offsets, kernels, reg_weight, head_weight, depth_cot):
    vmem = pl.BlockSpec(memory_space=pltpu.VMEM)
    smem = pl.BlockSpec(memory_space=pltpu.SMEM)
    hbm = pl.BlockSpec(memory_space=pltpu.HBM)
    dma = pltpu.SemaphoreType.DMA
    shape = jax.ShapeDtypeStruct

    win, index, cot, diag, band, columns = pl.pallas_call(
        exchange_kernel,
        name="exchange",
        out_shape=(
            shape((ZERO + 1, C, 128), bf16), shape((NF, 128), i32), shape((NF, 128), f32),
            shape((D // 2, 256, 256), bf16), shape((2 * D, D * C), bf16), shape((3, C, 128), f32),
        ),
        in_specs=[hbm] * 7,
        out_specs=(vmem,) * 6,
        scratch_shapes=[
            pltpu.VMEM((NB, C, 128), bf16),
            pltpu.VMEM((V, NB, D), i32),
            pltpu.VMEM((1, NB * 128), f32),
            pltpu.VMEM((3, 8, C), bf16),
            pltpu.SMEM((V, 16), i32),
            pltpu.SMEM((8,), f32),
            pltpu.VMEM((NB, 1, 256), f32),
            pltpu.VMEM((NF, 1, 256), f32),
            dma((NB,)), dma((NF,)), dma((NB,)), dma((NF,)), dma((4,)), dma((NF,)), dma((NF,)), dma((8,)),
        ],
        compiler_params=pltpu.CompilerParams(
            collective_id=0, has_side_effects=True, vmem_limit_bytes=16 << 20
        ),
    )(
        *(
            pltpu.with_memory_space_constraint(x, pltpu.HBM)
            for x in (
                features.reshape(C, NB * 128), jnp.transpose(offsets[0], (0, 2, 1)), depth_cot, views.T,
                kernels.reshape(D // 2, 2, 128, 128), reg_weight, head_weight,
            )
        )
    )

    depths, acc, ref_acc = pl.pallas_call(
        compute_kernel,
        name="compute",
        out_shape=(shape((NF, 1, 128), f32), shape((ZERO + 1, C, 128), f32), shape((NF, C, 128), f32)),
        in_specs=[smem] + [vmem] * 5,
        out_specs=(vmem,) * 3,
        scratch_shapes=[
            pltpu.VMEM((D, NF, V + 1, C, 128), bf16),
            pltpu.VMEM((D * C, NF * 128), bf16),
            pltpu.VMEM((NF, D, 128), f32),
        ],
        compiler_params=pltpu.CompilerParams(vmem_limit_bytes=40 << 20),
    )(index, win, diag, band, columns, cot)

    depth_rx, rx = pl.pallas_call(
        return_kernel,
        name="give_back",
        out_shape=(shape((NB, 1, 128), f32), shape((NB + 4, W, C, 128), bf16)),
        in_specs=[vmem] * 3,
        out_specs=(vmem,) * 2,
        scratch_shapes=[
            pltpu.VMEM((NF * W, C, 128), bf16),
            pltpu.VMEM((NF * W, C, 128), bf16),
            pltpu.VMEM((NF * W, C, 128), bf16),
            dma((NF,)), dma((NB + 4,)), dma((NF,)), dma((NF,)), dma((NB,)), dma((NF,)), dma((NF,)),
        ],
        compiler_params=pltpu.CompilerParams(
            collective_id=1, has_side_effects=True, vmem_limit_bytes=16 << 20
        ),
    )(acc, ref_acc, depths)

    depth_map, grad = pl.pallas_call(
        sum_kernel,
        name="total",
        out_shape=(shape((1, NB * 128), f32), shape((C, NB * 128), f32)),
        in_specs=[vmem] * 2,
        out_specs=(vmem,) * 2,
        compiler_params=pltpu.CompilerParams(vmem_limit_bytes=8 << 20),
    )(depth_rx, rx)
    return depth_map, grad.reshape(1, C, NB * 128)


def solution(mesh):
    return jax.shard_map(
        per_device,
        mesh=mesh,
        in_specs=(
            P("frame", None, "tile"),
            P(),
            P("frame", None, None, "tile"),
            P(),
            P(),
            P(),
            P("frame", "tile"),
        ),
        out_specs=(P("frame", "tile"), P("frame", None, "tile")),
        check_vma=False,
    )
```

```python
import functools

import jax
import jax.numpy as jnp
from jax import lax
from jax.experimental import pallas as pl
from jax.experimental.pallas import tpu as pltpu
from jax.sharding import PartitionSpec as P

MESH = pl.DeviceIdType.MESH
f32, bf16, i32 = jnp.float32, jnp.bfloat16, jnp.int32

C = 32
D = 32
V = 4
NF = 8
NB = 8
W = 5
ZERO = 2 * NF * W

PARTS = ((0, 0, 2, 3), (1, 1, 1, 4), (2, 5, 0, 5), (6, 6, 0, 4), (7, 7, 0, 3))


def place():
    frame = lax.axis_index("frame")
    tile = lax.axis_index("tile")
    core = frame % 2
    own = frame // 2
    return frame, core, own, (own % 4) * 2 + own // 4, tile, lax.axis_size("tile")


def frame_at(block, core):
    return (block % 2) * 8 + (block // 2) * 2 + core


def signal(semaphore, frame, tile):
    pl.semaphore_signal(semaphore, inc=1, device_id=(frame, tile), device_id_type=MESH)


def remote(src, dst, send, recv, frame, tile):
    return pltpu.make_async_remote_copy(
        src_ref=src, dst_ref=dst, send_sem=send, recv_sem=recv, device_id=(frame, tile), device_id_type=MESH
    )


def wait_bytes(ref, semaphore):
    pltpu.make_async_copy(ref, ref, semaphore).wait()


def make_bands(taps, head, band, columns):
    rows = []
    for t in range(3):
        tap = taps[t].astype(f32)
        rows.append(sum(head[r] * tap[r:r + 1, :] for r in range(8)))
    row_id = lax.broadcasted_iota(i32, (8, C), 0)
    weight = jnp.where(row_id == 0, rows[0], jnp.where(row_id == 1, rows[1], jnp.where(row_id == 2, rows[2], 0.0)))
    w_hi = weight.astype(bf16)
    w_lo = (weight - w_hi.astype(f32)).astype(bf16)
    wide_lane = lax.broadcasted_iota(i32, (C, D * C), 1)
    wide_row = lax.broadcasted_iota(i32, (C, D * C), 0)
    spread = (wide_lane % C == wide_row).astype(f32).astype(bf16)
    tap_of = wide_lane // C - wide_row + 1
    bands = []
    for part in (w_hi, w_lo):
        wide = jnp.dot(part, spread, preferred_element_type=f32)
        bands.append(sum(jnp.where(tap_of == t, wide[t:t + 1, :], 0.0) for t in range(3)))
    band[...] = jnp.concatenate(bands, axis=0).astype(bf16)
    upright = jnp.transpose(jnp.concatenate([weight, jnp.zeros((8, 128 - C), f32)], axis=1))
    for t in range(3):
        columns[t] = jnp.broadcast_to(upright[:C, t:t + 1], (C, 128))


def exchange_kernel(
    feats, offsets_hbm, cot_hbm, views_hbm, kernels, taps_hbm, head_hbm,
    win, index_out, cot_out, diag, band, columns,
    blocks, offsets, cot, taps, views, head, aux, aux_rx,
    send, recv, aux_send, aux_recv, rim_send, sib_send, sib_recv, load,
):
    frame, core, own, mine, tile, tiles = place()
    before, after = (tile + tiles - 1) % tiles, (tile + 1) % tiles
    sibling = frame + 1 - 2 * core

    barrier = pltpu.get_barrier_semaphore()

    has_before, has_after = tile > 0, tile < tiles - 1
    edge = ((mine < 2) & (tile == 0)) | ((mine > 5) & (tile == tiles - 1))

    @pl.when((mine < 2) & has_before)
    def _():
        def greet_before(b, carry):
            signal(barrier, frame_at(b, core), before)
            return carry

        lax.fori_loop(0, NB, greet_before, 0)

    @pl.when((mine > 5) & has_after)
    def _():
        def greet_after(b, carry):
            signal(barrier, frame_at(b, core), after)
            return carry

        lax.fori_loop(0, NB, greet_after, 0)

    def greet(s, carry):
        signal(barrier, frame_at((mine + s) % NB, core), tile)
        return carry

    lax.fori_loop(1, NB, greet, 0)

    signal(barrier, sibling, tile)

    for b in range(NB):
        pltpu.make_async_copy(feats.at[:, pl.ds(b * 128, 128)], blocks.at[b], load.at[0]).start()
    small = [
        pltpu.make_async_copy(src, dst, load.at[n])
        for n, (src, dst) in enumerate(
            ((offsets_hbm, offsets), (cot_hbm, cot), (views_hbm, views), (taps_hbm, taps), (head_hbm, head)), 1
        )
    ]
    half = [
        pltpu.make_async_copy(
            kernels.at[:, h], diag.at[:, pl.ds(h * 128, 128), pl.ds(h * 128, 128)], load.at[6 + h]
        )
        for h in range(2)
    ]
    for copy in small:
        copy.start()
    for copy in half:
        copy.start()
    win[ZERO] = jnp.zeros((C, 128), bf16)
    for b, outside in ((0, (0, 1)), (1, (0,)), (6, (4,)), (7, (3, 4))):
        @pl.when((mine == b) & edge)
        def _():
            for i in range(NF):
                for k in outside:
                    win[i * W + k] = jnp.zeros((C, 128), bf16)

    small[0].wait()
    small[1].wait()
    for b in range(NB):
        for j in range(V):
            aux[b, :, j * D:(j + 1) * D] = offsets[j, b:b + 1, :].astype(f32)
        aux[b, :, 128:256] = cot[:, b * 128:(b + 1) * 128]
    wait_bytes(blocks, load.at[0])

    pl.semaphore_wait(barrier, NB + jnp.where(has_before, 2, 0) + jnp.where(has_after, 2, 0))

    rims = (
        (0, 1, 4, 6, before, has_before), (0, 2, 3, 7, before, has_before),
        (6, 2, 0, 0, after, has_after), (7, 1, 0, 1, after, has_after),
    )
    rim_copies = [
        (
            remote(
                blocks.at[pl.ds(first, count)], win.at[pl.ds(own * W + at, count)],
                rim_send.at[n], recv.at[own], frame_at(b, core), where,
            ),
            there,
        )
        for n, (first, count, at, b, where, there) in enumerate(rims)
    ]
    for copy, there in rim_copies:
        @pl.when(there)
        def _():
            copy.start()

    def part_copy(b, at, count):
        return remote(
            blocks.at[pl.ds(b - 2 + at, count)], win.at[pl.ds(own * W + at, count)],
            send.at[b], recv.at[own], frame_at(b, core), tile,
        )

    def aux_copy(b):
        return remote(aux.at[b], aux_rx.at[own], aux_send.at[b], aux_recv.at[own], frame_at(b, core), tile)

    def start(n, carry):
        b = (mine + jnp.where(n % 2 == 1, 4 - (n + 1) // 2, 4 + n // 2)) % NB
        aux_copy(b).start()
        for least, most, at, count in PARTS:
            @pl.when((b >= least) & (b <= most))
            def _():
                part_copy(b, at, count).start()
        return carry

    lax.fori_loop(0, NB - 1, start, 0)
    pltpu.make_async_copy(aux.at[mine], aux_rx.at[own], aux_recv.at[own]).start()
    for least, most, at, count in PARTS:
        @pl.when((mine >= least) & (mine <= most))
        def _():
            pltpu.make_async_copy(
                blocks.at[pl.ds(mine - 2 + at, count)], win.at[pl.ds(own * W + at, count)], recv.at[own]
            ).start()

    corner = jnp.zeros((D // 2, 128, 128), bf16)
    diag[:, 0:128, 128:256] = corner
    diag[:, 128:256, 0:128] = corner
    for copy in small[2:]:
        copy.wait()
    make_bands(taps, head, band, columns)

    def window(i):
        return win.at[pl.ds(i * W, W)]

    def to_sibling(i):
        return remote(
            window(i), window(NF + i), sib_send.at[i], sib_recv.at[i], sibling, tile
        )

    def forward(s, carry):
        i = (own + s) % NF
        @pl.when(jnp.logical_not(edge))
        def _():
            wait_bytes(window(i), recv.at[i])

        for b, _, at, count in PARTS:
            if count < W:
                @pl.when((mine == b) & edge)
                def _():
                    wait_bytes(win.at[pl.ds(i * W + at, count)], recv.at[i])
        to_sibling(i).start()
        return carry

    lax.fori_loop(0, NF, forward, 0)

    view_of = lax.broadcasted_iota(i32, (1, 128), 1) // D
    here = tile * NB + mine
    for i in range(NF):
        wait_bytes(aux_rx.at[i], aux_recv.at[i])
        shift = aux_rx[i, :, 0:128].astype(i32)
        at = here + shift
        row = jnp.zeros((1, 128), i32)
        for j in range(V):
            v = views[j, 2 * i + core]
            row = jnp.where(view_of == j, jnp.where(v % 2 == core, 0, NF * W) + (v // 2) * W + 2, row)
        index_out[i:i + 1, :] = jnp.where((at >= 0) & (at < tiles * NB), row + shift, ZERO)
        cot_out[i:i + 1, :] = aux_rx[i, :, 128:256]

    def settle(s, carry):
        b = (mine + s) % NB
        aux_copy(b).wait_send()
        for least, most, at, count in PARTS:
            @pl.when((b >= least) & (b <= most))
            def _():
                part_copy(b, at, count).wait_send()
        return carry

    lax.fori_loop(1, NB, settle, 0)
    for copy, there in rim_copies:
        @pl.when(there)
        def _():
            copy.wait_send()

    def settle_sibling(i, carry):
        to_sibling(i).wait_send()
        wait_bytes(window(NF + i), sib_recv.at[i])
        return carry

    lax.fori_loop(0, NF, settle_sibling, 0)
    for copy in half:
        copy.wait()


def compute_kernel(idx, win, diag, band, columns, cot, depth_out, acc, ref_acc, cen, vd, d_pre):
    step = 2
    mean_of = 1.0 / (V + 1)

    for p in range(D // 2):
        mat = diag[p]
        for i0 in range(0, NF, step):
            picks = [
                jnp.concatenate([win[idx[i, j * D + 2 * p + h]] for h in range(2)], axis=1)
                for i in range(i0, i0 + step) for j in range(V)
            ]
            y = jnp.dot(jnp.concatenate(picks, axis=0), mat, preferred_element_type=f32)
            for i in range(i0, i0 + step):
                for h in range(2):
                    o, d = (i - i0) * V * C, 2 * p + h
                    xs = [win[i * W + 2].astype(f32)]
                    xs += [y[o + j * C:o + (j + 1) * C, h * 128:(h + 1) * 128] for j in range(V)]
                    average = (((xs[0] + xs[1]) + (xs[2] + xs[3])) + xs[4]) * mean_of
                    cs = [x - average for x in xs]
                    sq = [c * c for c in cs]
                    variance = (((sq[0] + sq[1]) + (sq[2] + sq[3])) + sq[4]) * mean_of
                    vd[d * C:(d + 1) * C, i * 128:(i + 1) * 128] = variance.astype(bf16)
                    for j in range(V + 1):
                        cen[d, i, j] = cs[j].astype(bf16)

    value = (lax.broadcasted_iota(i32, (D, 128), 0).astype(f32) + 1.0) / D
    for i0 in range(0, NF, 2):
        both = jnp.dot(band[...], vd[:, i0 * 128:(i0 + 2) * 128], preferred_element_type=f32)
        for i in range(i0, i0 + 2):
            o = (i - i0) * 128
            th = jnp.tanh(both[:D, o:o + 128] + both[D:, o:o + 128])
            w = jnp.exp(4.0 * th)
            total = jnp.sum(w, axis=0, keepdims=True)
            depth = jnp.sum(w * value, axis=0, keepdims=True) / total
            depth_out[i] = depth
            scale = cot[i:i + 1, :] / total * (4.0 * 2.0 / (V + 1))
            d_pre[i] = (w * (value - depth)) * scale * (1.0 - th * th)

    acc[...] = jnp.zeros_like(acc)
    ref_acc[...] = jnp.zeros_like(ref_acc)

    for p in range(D // 2):
        mat = diag[p]
        for i0 in range(0, NF, step):
            gs = []
            for i in range(i0, i0 + step):
                dvs = []
                for d in (2 * p, 2 * p + 1):
                    terms = [columns[t] * d_pre[i, d - t + 1:d - t + 2, :] for t in range(3) if 0 <= d - t + 1 < D]
                    dvs.append(sum(terms[1:], terms[0]).astype(bf16))
                ref_acc[i] += (dvs[0] * cen[2 * p, i, 0]).astype(f32) + (dvs[1] * cen[2 * p + 1, i, 0]).astype(f32)
                for j in range(V):
                    gs.append(jnp.concatenate([dvs[h] * cen[2 * p + h, i, j + 1] for h in range(2)], axis=1))
            y = lax.dot_general(
                jnp.concatenate(gs, axis=0), mat, (((1,), (1,)), ((), ())), preferred_element_type=f32
            )
            for h in range(2):
                for i in range(i0, i0 + step):
                    slots = [idx[i, j * D + 2 * p + h] for j in range(V)]
                    o = (i - i0) * V * C
                    new = [acc[slots[j]] + y[o + j * C:o + (j + 1) * C, h * 128:(h + 1) * 128] for j in range(V)]
                    for j in range(V):
                        acc[slots[j]] = new[j]


def return_kernel(
    acc, ref_acc, depths, depth_rx, rx,
    grad_sib, sib_rx, out, send, recv, rim_send, depth_send, depth_recv, sib_send, sib_recv,
):
    frame, core, own, mine, tile, tiles = place()
    before, after = (tile + tiles - 1) % tiles, (tile + 1) % tiles
    sibling = frame + 1 - 2 * core

    barrier = pltpu.get_barrier_semaphore()
    has_before, has_after = tile > 0, tile < tiles - 1

    @pl.when(has_before)
    def _():
        for b in (6, 7):
            signal(barrier, frame_at(b, core), before)

    @pl.when(has_after)
    def _():
        for b in (0, 1):
            signal(barrier, frame_at(b, core), after)

    signal(barrier, sibling, tile)

    def greet(s, carry):
        signal(barrier, frame_at((mine + s) % NB, core), tile)
        return carry

    lax.fori_loop(1, NB, greet, 0)

    outer = [
        (slot, first - slot + 4, last - first + 1, has_before if slot < 2 else has_after)
        for slot in (0, 1, NB + 2, NB + 3)
        for first, last in [(max(slot - 4, 0), min(slot, NB - 1))]
    ]
    for slot, at, count, there in outer:
        @pl.when(jnp.logical_not(there))
        def _():
            for k in range(at, at + count):
                rx[slot, k] = jnp.zeros((C, 128), bf16)

    for s in range(NF * W):
        grad_sib[s] = acc[NF * W + s].astype(bf16)

    pl.semaphore_wait(barrier, jnp.where(((mine < 2) & has_before) | ((mine > 5) & has_after), 2 * NB, NB))

    def window(ref, i):
        return ref.at[pl.ds(i * W, W)]

    def to_sibling(i):
        return remote(
            window(grad_sib, i), window(sib_rx, i), sib_send.at[i], sib_recv.at[i], sibling, tile
        )

    def owner(n):
        across, along = 1 - n % 2, jnp.where(n < 2, 2, jnp.where(n < 4, 1, jnp.where(n < 6, 3, 0)))
        return ((own // 4 + across) % 2) * 4 + (own % 4 + along) % 4

    def start_sibling(n, carry):
        to_sibling(owner(n)).start()
        return carry

    lax.fori_loop(0, NF, start_sibling, 0)

    def part_copy(i, at, count):
        return remote(
            out.at[pl.ds(i * W + at, count)], rx.at[mine + 2, pl.ds(at, count)],
            send.at[i], recv.at[mine + 2], 2 * i + core, tile,
        )

    def rim_copy(i, at, count, slot, where):
        return remote(
            out.at[pl.ds(i * W + at, count)], rx.at[slot, pl.ds(at, count)],
            rim_send.at[i], recv.at[slot], 2 * i + core, where,
        )

    def depth_copy(i):
        return remote(
            depths.at[i], depth_rx.at[mine], depth_send.at[i], depth_recv.at[mine], 2 * i + core, tile
        )

    rims = (
        (0, 0, 2, 10, before, has_before), (1, 0, 1, 11, before, has_before),
        (6, 4, 1, 0, after, has_after), (7, 3, 2, 1, after, has_after),
    )

    def send_parts(i):
        @pl.when(i != own)
        def _():
            depth_copy(i).start()
            for least, most, at, count in PARTS:
                @pl.when((mine >= least) & (mine <= most))
                def _():
                    part_copy(i, at, count).start()

    at_edge = (mine < 2) | (mine > 5)

    def add_and_send(n, carry):
        i = owner(n)
        wait_bytes(window(sib_rx, i), sib_recv.at[i])
        for k in range(W):
            total = acc[i * W + k] + sib_rx[i * W + k].astype(f32)
            out[i * W + k] = (total + ref_acc[i] if k == 2 else total).astype(bf16)
        for b, at, count, slot, where, there in rims:
            @pl.when((mine == b) & there)
            def _():
                rim_copy(i, at, count, slot, where).start()

        @pl.when(jnp.logical_not(at_edge))
        def _():
            send_parts(i)

        return carry

    lax.fori_loop(0, NF, add_and_send, 0)

    @pl.when(at_edge)
    def _():
        def send_later(n, carry):
            send_parts(owner(n))
            return carry

        lax.fori_loop(0, NF, send_later, 0)

    pltpu.make_async_copy(depths.at[own], depth_rx.at[mine], depth_recv.at[mine]).start()
    for least, most, at, count in PARTS:
        @pl.when((mine >= least) & (mine <= most))
        def _():
            pltpu.make_async_copy(
                out.at[pl.ds(own * W + at, count)], rx.at[mine + 2, pl.ds(at, count)], recv.at[mine + 2]
            ).start()

    for b in range(NB):
        wait_bytes(depth_rx.at[b], depth_recv.at[b])
    for slot in range(2, NB + 2):
        first, last = max(slot - 4, 0), min(slot, NB - 1)
        wait_bytes(rx.at[slot, pl.ds(first - slot + 4, last - first + 1)], recv.at[slot])
    for slot, at, count, there in outer:
        @pl.when(there)
        def _():
            wait_bytes(rx.at[slot, pl.ds(at, count)], recv.at[slot])

    def settle(s, carry):
        i = (own + s) % NF
        to_sibling(i).wait_send()
        for b, at, count, slot, where, there in rims:
            @pl.when((mine == b) & there)
            def _():
                rim_copy(i, at, count, slot, where).wait_send()

        @pl.when(i != own)
        def _():
            depth_copy(i).wait_send()
            for least, most, at, count in PARTS:
                @pl.when((mine >= least) & (mine <= most))
                def _():
                    part_copy(i, at, count).wait_send()

        return carry

    lax.fori_loop(1, NF + 1, settle, 0)


def sum_kernel(depth_rx, rx, depth_out, grad_out):
    for b in range(NB):
        depth_out[:, b * 128:(b + 1) * 128] = depth_rx[b]
        total = rx[b, 4].astype(f32)
        for k in range(1, W):
            total += rx[b + k, 4 - k].astype(f32)
        grad_out[:, b * 128:(b + 1) * 128] = total


def per_device(features, views, offsets, kernels, reg_weight, head_weight, depth_cot):
    vmem = pl.BlockSpec(memory_space=pltpu.VMEM)
    smem = pl.BlockSpec(memory_space=pltpu.SMEM)
    hbm = pl.BlockSpec(memory_space=pltpu.HBM)
    dma = pltpu.SemaphoreType.DMA
    shape = jax.ShapeDtypeStruct

    win, index, cot, diag, band, columns = pl.pallas_call(
        exchange_kernel,
        name="exchange",
        out_shape=(
            shape((ZERO + 1, C, 128), bf16), shape((NF, 128), i32), shape((NF, 128), f32),
            shape((D // 2, 256, 256), bf16), shape((2 * D, D * C), bf16), shape((3, C, 128), f32),
        ),
        in_specs=[hbm] * 7,
        out_specs=(vmem,) * 6,
        scratch_shapes=[
            pltpu.VMEM((NB, C, 128), bf16),
            pltpu.VMEM((V, NB, D), i32),
            pltpu.VMEM((1, NB * 128), f32),
            pltpu.VMEM((3, 8, C), bf16),
            pltpu.SMEM((V, 16), i32),
            pltpu.SMEM((8,), f32),
            pltpu.VMEM((NB, 1, 256), f32),
            pltpu.VMEM((NF, 1, 256), f32),
            dma((NB,)), dma((NF,)), dma((NB,)), dma((NF,)), dma((4,)), dma((NF,)), dma((NF,)), dma((8,)),
        ],
        compiler_params=pltpu.CompilerParams(
            collective_id=0, has_side_effects=True, vmem_limit_bytes=16 << 20
        ),
    )(
        *(
            pltpu.with_memory_space_constraint(x, pltpu.HBM)
            for x in (
                features.reshape(C, NB * 128), jnp.transpose(offsets[0], (0, 2, 1)), depth_cot, views.T,
                kernels.reshape(D // 2, 2, 128, 128), reg_weight, head_weight,
            )
        )
    )

    depths, acc, ref_acc = pl.pallas_call(
        compute_kernel,
        name="compute",
        out_shape=(shape((NF, 1, 128), f32), shape((ZERO + 1, C, 128), f32), shape((NF, C, 128), f32)),
        in_specs=[smem] + [vmem] * 5,
        out_specs=(vmem,) * 3,
        scratch_shapes=[
            pltpu.VMEM((D, NF, V + 1, C, 128), bf16),
            pltpu.VMEM((D * C, NF * 128), bf16),
            pltpu.VMEM((NF, D, 128), f32),
        ],
        compiler_params=pltpu.CompilerParams(vmem_limit_bytes=40 << 20),
    )(index, win, diag, band, columns, cot)

    depth_rx, rx = pl.pallas_call(
        return_kernel,
        name="give_back",
        out_shape=(shape((NB, 1, 128), f32), shape((NB + 4, W, C, 128), bf16)),
        in_specs=[vmem] * 3,
        out_specs=(vmem,) * 2,
        scratch_shapes=[
            pltpu.VMEM((NF * W, C, 128), bf16),
            pltpu.VMEM((NF * W, C, 128), bf16),
            pltpu.VMEM((NF * W, C, 128), bf16),
            dma((NF,)), dma((NB + 4,)), dma((NF,)), dma((NF,)), dma((NB,)), dma((NF,)), dma((NF,)),
        ],
        compiler_params=pltpu.CompilerParams(
            collective_id=1, has_side_effects=True, vmem_limit_bytes=16 << 20
        ),
    )(acc, ref_acc, depths)

    depth_map, grad = pl.pallas_call(
        sum_kernel,
        name="total",
        out_shape=(shape((1, NB * 128), f32), shape((C, NB * 128), f32)),
        in_specs=[vmem] * 2,
        out_specs=(vmem,) * 2,
        compiler_params=pltpu.CompilerParams(vmem_limit_bytes=8 << 20),
    )(depth_rx, rx)
    return depth_map, grad.reshape(1, C, NB * 128)


def solution(mesh):
    return jax.shard_map(
        per_device,
        mesh=mesh,
        in_specs=(
            P("frame", None, "tile"),
            P(),
            P("frame", None, None, "tile"),
            P(),
            P(),
            P(),
            P("frame", "tile"),
        ),
        out_specs=(P("frame", "tile"), P("frame", None, "tile")),
        check_vma=False,
    )
```

```python
import functools

import jax
import jax.numpy as jnp
from jax import lax
from jax.experimental import pallas as pl
from jax.experimental.pallas import tpu as pltpu
from jax.sharding import PartitionSpec as P

MESH = pl.DeviceIdType.MESH
f32, bf16, i32 = jnp.float32, jnp.bfloat16, jnp.int32

C = 32
D = 32
V = 4
NF = 8
NB = 8
W = 5
ZERO = 2 * NF * W

PARTS = ((0, 0, 2, 3), (1, 1, 1, 4), (2, 5, 0, 5), (6, 6, 0, 4), (7, 7, 0, 3))


def place():
    frame = lax.axis_index("frame")
    tile = lax.axis_index("tile")
    core = frame % 2
    own = frame // 2
    return frame, core, own, (own % 4) * 2 + own // 4, tile, lax.axis_size("tile")


def frame_at(block, core):
    return (block % 2) * 8 + (block // 2) * 2 + core


def signal(semaphore, frame, tile):
    pl.semaphore_signal(semaphore, inc=1, device_id=(frame, tile), device_id_type=MESH)


def remote(src, dst, send, recv, frame, tile):
    return pltpu.make_async_remote_copy(
        src_ref=src, dst_ref=dst, send_sem=send, recv_sem=recv, device_id=(frame, tile), device_id_type=MESH
    )


def wait_bytes(ref, semaphore):
    pltpu.make_async_copy(ref, ref, semaphore).wait()


def make_bands(taps, head, band, columns):
    rows = []
    for t in range(3):
        tap = taps[t].astype(f32)
        rows.append(sum(head[r] * tap[r:r + 1, :] for r in range(8)))
    row_id = lax.broadcasted_iota(i32, (8, C), 0)
    weight = jnp.where(row_id == 0, rows[0], jnp.where(row_id == 1, rows[1], jnp.where(row_id == 2, rows[2], 0.0)))
    w_hi = weight.astype(bf16)
    w_lo = (weight - w_hi.astype(f32)).astype(bf16)
    wide_lane = lax.broadcasted_iota(i32, (C, D * C), 1)
    wide_row = lax.broadcasted_iota(i32, (C, D * C), 0)
    spread = (wide_lane % C == wide_row).astype(f32).astype(bf16)
    tap_of = wide_lane // C - wide_row + 1
    bands = []
    for part in (w_hi, w_lo):
        wide = jnp.dot(part, spread, preferred_element_type=f32)
        bands.append(sum(jnp.where(tap_of == t, wide[t:t + 1, :], 0.0) for t in range(3)))
    band[...] = jnp.concatenate(bands, axis=0).astype(bf16)
    upright = jnp.transpose(jnp.concatenate([weight, jnp.zeros((8, 128 - C), f32)], axis=1))
    for t in range(3):
        columns[t] = jnp.broadcast_to(upright[:C, t:t + 1], (C, 128))


def exchange_kernel(
    feats, offsets_hbm, cot_hbm, views_hbm, kernels, taps_hbm, head_hbm,
    win, index_out, cot_out, diag, band, columns,
    blocks, offsets, cot, taps, views, head, aux, aux_rx,
    send, recv, aux_send, aux_recv, rim_send, sib_send, sib_recv, load,
):
    frame, core, own, mine, tile, tiles = place()
    before, after = (tile + tiles - 1) % tiles, (tile + 1) % tiles
    sibling = frame + 1 - 2 * core

    barrier = pltpu.get_barrier_semaphore()

    has_before, has_after = tile > 0, tile < tiles - 1
    edge = ((mine < 2) & (tile == 0)) | ((mine > 5) & (tile == tiles - 1))

    @pl.when((mine < 2) & has_before)
    def _():
        def greet_before(b, carry):
            signal(barrier, frame_at(b, core), before)
            return carry

        lax.fori_loop(0, NB, greet_before, 0)

    @pl.when((mine > 5) & has_after)
    def _():
        def greet_after(b, carry):
            signal(barrier, frame_at(b, core), after)
            return carry

        lax.fori_loop(0, NB, greet_after, 0)


    for b in range(NB):
        pltpu.make_async_copy(feats.at[:, pl.ds(b * 128, 128)], blocks.at[b], load.at[0]).start()
    small = [
        pltpu.make_async_copy(src, dst, load.at[n])
        for n, (src, dst) in enumerate(
            ((offsets_hbm, offsets), (cot_hbm, cot), (views_hbm, views), (taps_hbm, taps), (head_hbm, head)), 1
        )
    ]
    half = [
        pltpu.make_async_copy(
            kernels.at[:, h], diag.at[:, pl.ds(h * 128, 128), pl.ds(h * 128, 128)], load.at[6 + h]
        )
        for h in range(2)
    ]
    for copy in small:
        copy.start()
    def greet(s, carry):
        signal(barrier, frame_at((mine + s) % NB, core), tile)
        return carry

    lax.fori_loop(1, NB, greet, 0)

    signal(barrier, sibling, tile)
    win[ZERO] = jnp.zeros((C, 128), bf16)
    for b, outside in ((0, (0, 1)), (1, (0,)), (6, (4,)), (7, (3, 4))):
        @pl.when((mine == b) & edge)
        def _():
            for i in range(NF):
                for k in outside:
                    win[i * W + k] = jnp.zeros((C, 128), bf16)

    small[0].wait()
    small[1].wait()
    for b in range(NB):
        for j in range(V):
            aux[b, :, j * D:(j + 1) * D] = offsets[j, b:b + 1, :].astype(f32)
        aux[b, :, 128:256] = cot[:, b * 128:(b + 1) * 128]
    wait_bytes(blocks, load.at[0])

    pl.semaphore_wait(barrier, NB + jnp.where(has_before, 2, 0) + jnp.where(has_after, 2, 0))

    rims = (
        (0, 1, 4, 6, before, has_before), (0, 2, 3, 7, before, has_before),
        (6, 2, 0, 0, after, has_after), (7, 1, 0, 1, after, has_after),
    )
    rim_copies = [
        (
            remote(
                blocks.at[pl.ds(first, count)], win.at[pl.ds(own * W + at, count)],
                rim_send.at[n], recv.at[own], frame_at(b, core), where,
            ),
            there,
        )
        for n, (first, count, at, b, where, there) in enumerate(rims)
    ]
    for copy, there in rim_copies:
        @pl.when(there)
        def _():
            copy.start()

    def part_copy(b, at, count):
        return remote(
            blocks.at[pl.ds(b - 2 + at, count)], win.at[pl.ds(own * W + at, count)],
            send.at[b], recv.at[own], frame_at(b, core), tile,
        )

    def aux_copy(b):
        return remote(aux.at[b], aux_rx.at[own], aux_send.at[b], aux_recv.at[own], frame_at(b, core), tile)

    def start(n, carry):
        b = (mine + jnp.where(n % 2 == 1, 4 - (n + 1) // 2, 4 + n // 2)) % NB
        aux_copy(b).start()
        for least, most, at, count in PARTS:
            @pl.when((b >= least) & (b <= most))
            def _():
                part_copy(b, at, count).start()
        return carry

    lax.fori_loop(0, NB - 1, start, 0)
    pltpu.make_async_copy(aux.at[mine], aux_rx.at[own], aux_recv.at[own]).start()
    for least, most, at, count in PARTS:
        @pl.when((mine >= least) & (mine <= most))
        def _():
            pltpu.make_async_copy(
                blocks.at[pl.ds(mine - 2 + at, count)], win.at[pl.ds(own * W + at, count)], recv.at[own]
            ).start()

    for copy in half:
        copy.start()
    corner = jnp.zeros((D // 2, 128, 128), bf16)
    diag[:, 0:128, 128:256] = corner
    diag[:, 128:256, 0:128] = corner
    for copy in small[2:]:
        copy.wait()
    make_bands(taps, head, band, columns)

    def window(i):
        return win.at[pl.ds(i * W, W)]

    def to_sibling(i):
        return remote(
            window(i), window(NF + i), sib_send.at[i], sib_recv.at[i], sibling, tile
        )

    def forward(s, carry):
        i = (own + s) % NF
        @pl.when(jnp.logical_not(edge))
        def _():
            wait_bytes(window(i), recv.at[i])

        for b, _, at, count in PARTS:
            if count < W:
                @pl.when((mine == b) & edge)
                def _():
                    wait_bytes(win.at[pl.ds(i * W + at, count)], recv.at[i])
        to_sibling(i).start()
        return carry

    lax.fori_loop(0, NF, forward, 0)

    view_of = lax.broadcasted_iota(i32, (1, 128), 1) // D
    here = tile * NB + mine
    for i in range(NF):
        wait_bytes(aux_rx.at[i], aux_recv.at[i])
        shift = aux_rx[i, :, 0:128].astype(i32)
        at = here + shift
        row = jnp.zeros((1, 128), i32)
        for j in range(V):
            v = views[j, 2 * i + core]
            row = jnp.where(view_of == j, jnp.where(v % 2 == core, 0, NF * W) + (v // 2) * W + 2, row)
        index_out[i:i + 1, :] = jnp.where((at >= 0) & (at < tiles * NB), row + shift, ZERO)
        cot_out[i:i + 1, :] = aux_rx[i, :, 128:256]

    def settle(s, carry):
        b = (mine + s) % NB
        aux_copy(b).wait_send()
        for least, most, at, count in PARTS:
            @pl.when((b >= least) & (b <= most))
            def _():
                part_copy(b, at, count).wait_send()
        return carry

    lax.fori_loop(1, NB, settle, 0)
    for copy, there in rim_copies:
        @pl.when(there)
        def _():
            copy.wait_send()

    def settle_sibling(i, carry):
        to_sibling(i).wait_send()
        wait_bytes(window(NF + i), sib_recv.at[i])
        return carry

    lax.fori_loop(0, NF, settle_sibling, 0)
    for copy in half:
        copy.wait()


def compute_kernel(idx, win, diag, band, columns, cot, depth_out, acc, ref_acc, cen, vd, d_pre):
    step = 2
    mean_of = 1.0 / (V + 1)

    for p in range(D // 2):
        mat = diag[p]
        for i0 in range(0, NF, step):
            picks = [
                jnp.concatenate([win[idx[i, j * D + 2 * p + h]] for h in range(2)], axis=1)
                for i in range(i0, i0 + step) for j in range(V)
            ]
            y = jnp.dot(jnp.concatenate(picks, axis=0), mat, preferred_element_type=f32)
            for i in range(i0, i0 + step):
                for h in range(2):
                    o, d = (i - i0) * V * C, 2 * p + h
                    xs = [win[i * W + 2].astype(f32)]
                    xs += [y[o + j * C:o + (j + 1) * C, h * 128:(h + 1) * 128] for j in range(V)]
                    average = (((xs[0] + xs[1]) + (xs[2] + xs[3])) + xs[4]) * mean_of
                    cs = [x - average for x in xs]
                    sq = [c * c for c in cs]
                    variance = (((sq[0] + sq[1]) + (sq[2] + sq[3])) + sq[4]) * mean_of
                    vd[d * C:(d + 1) * C, i * 128:(i + 1) * 128] = variance.astype(bf16)
                    for j in range(V + 1):
                        cen[d, i, j] = cs[j].astype(bf16)

    value = (lax.broadcasted_iota(i32, (D, 128), 0).astype(f32) + 1.0) / D
    for i0 in range(0, NF, 2):
        both = jnp.dot(band[...], vd[:, i0 * 128:(i0 + 2) * 128], preferred_element_type=f32)
        for i in range(i0, i0 + 2):
            o = (i - i0) * 128
            th = jnp.tanh(both[:D, o:o + 128] + both[D:, o:o + 128])
            w = jnp.exp(4.0 * th)
            total = jnp.sum(w, axis=0, keepdims=True)
            depth = jnp.sum(w * value, axis=0, keepdims=True) / total
            depth_out[i] = depth
            scale = cot[i:i + 1, :] / total * (4.0 * 2.0 / (V + 1))
            d_pre[i] = (w * (value - depth)) * scale * (1.0 - th * th)

    acc[...] = jnp.zeros_like(acc)
    ref_acc[...] = jnp.zeros_like(ref_acc)

    for p in range(D // 2):
        mat = diag[p]
        for i0 in range(0, NF, step):
            gs = []
            for i in range(i0, i0 + step):
                dvs = []
                for d in (2 * p, 2 * p + 1):
                    terms = [columns[t] * d_pre[i, d - t + 1:d - t + 2, :] for t in range(3) if 0 <= d - t + 1 < D]
                    dvs.append(sum(terms[1:], terms[0]).astype(bf16))
                ref_acc[i] += (dvs[0] * cen[2 * p, i, 0]).astype(f32) + (dvs[1] * cen[2 * p + 1, i, 0]).astype(f32)
                for j in range(V):
                    gs.append(jnp.concatenate([dvs[h] * cen[2 * p + h, i, j + 1] for h in range(2)], axis=1))
            y = lax.dot_general(
                jnp.concatenate(gs, axis=0), mat, (((1,), (1,)), ((), ())), preferred_element_type=f32
            )
            for h in range(2):
                for i in range(i0, i0 + step):
                    slots = [idx[i, j * D + 2 * p + h] for j in range(V)]
                    o = (i - i0) * V * C
                    new = [acc[slots[j]] + y[o + j * C:o + (j + 1) * C, h * 128:(h + 1) * 128] for j in range(V)]
                    for j in range(V):
                        acc[slots[j]] = new[j]


def return_kernel(
    acc, ref_acc, depths, depth_rx, rx,
    grad_sib, sib_rx, out, send, recv, rim_send, depth_send, depth_recv, sib_send, sib_recv,
):
    frame, core, own, mine, tile, tiles = place()
    before, after = (tile + tiles - 1) % tiles, (tile + 1) % tiles
    sibling = frame + 1 - 2 * core

    barrier = pltpu.get_barrier_semaphore()
    has_before, has_after = tile > 0, tile < tiles - 1

    @pl.when(has_before)
    def _():
        for b in (6, 7):
            signal(barrier, frame_at(b, core), before)

    @pl.when(has_after)
    def _():
        for b in (0, 1):
            signal(barrier, frame_at(b, core), after)

    signal(barrier, sibling, tile)

    def greet(s, carry):
        signal(barrier, frame_at((mine + s) % NB, core), tile)
        return carry

    lax.fori_loop(1, NB, greet, 0)

    outer = [
        (slot, first - slot + 4, last - first + 1, has_before if slot < 2 else has_after)
        for slot in (0, 1, NB + 2, NB + 3)
        for first, last in [(max(slot - 4, 0), min(slot, NB - 1))]
    ]
    for slot, at, count, there in outer:
        @pl.when(jnp.logical_not(there))
        def _():
            for k in range(at, at + count):
                rx[slot, k] = jnp.zeros((C, 128), bf16)

    for s in range(NF * W):
        grad_sib[s] = acc[NF * W + s].astype(bf16)

    pl.semaphore_wait(barrier, jnp.where(((mine < 2) & has_before) | ((mine > 5) & has_after), 2 * NB, NB))

    def window(ref, i):
        return ref.at[pl.ds(i * W, W)]

    def to_sibling(i):
        return remote(
            window(grad_sib, i), window(sib_rx, i), sib_send.at[i], sib_recv.at[i], sibling, tile
        )

    def owner(n):
        across, along = 1 - n % 2, jnp.where(n < 2, 2, jnp.where(n < 4, 1, jnp.where(n < 6, 3, 0)))
        return ((own // 4 + across) % 2) * 4 + (own % 4 + along) % 4

    def start_sibling(n, carry):
        to_sibling(owner(n)).start()
        return carry

    lax.fori_loop(0, NF, start_sibling, 0)

    def part_copy(i, at, count):
        return remote(
            out.at[pl.ds(i * W + at, count)], rx.at[mine + 2, pl.ds(at, count)],
            send.at[i], recv.at[mine + 2], 2 * i + core, tile,
        )

    def rim_copy(i, at, count, slot, where):
        return remote(
            out.at[pl.ds(i * W + at, count)], rx.at[slot, pl.ds(at, count)],
            rim_send.at[i], recv.at[slot], 2 * i + core, where,
        )

    def depth_copy(i):
        return remote(
            depths.at[i], depth_rx.at[mine], depth_send.at[i], depth_recv.at[mine], 2 * i + core, tile
        )

    rims = (
        (0, 0, 2, 10, before, has_before), (1, 0, 1, 11, before, has_before),
        (6, 4, 1, 0, after, has_after), (7, 3, 2, 1, after, has_after),
    )

    def send_parts(i):
        @pl.when(i != own)
        def _():
            depth_copy(i).start()
            for least, most, at, count in PARTS:
                @pl.when((mine >= least) & (mine <= most))
                def _():
                    part_copy(i, at, count).start()

    at_edge = (mine < 2) | (mine > 5)

    def add_and_send(n, carry):
        i = owner(n)
        wait_bytes(window(sib_rx, i), sib_recv.at[i])
        for k in range(W):
            total = acc[i * W + k] + sib_rx[i * W + k].astype(f32)
            out[i * W + k] = (total + ref_acc[i] if k == 2 else total).astype(bf16)
        for b, at, count, slot, where, there in rims:
            @pl.when((mine == b) & there)
            def _():
                rim_copy(i, at, count, slot, where).start()

        @pl.when(jnp.logical_not(at_edge))
        def _():
            send_parts(i)

        return carry

    lax.fori_loop(0, NF, add_and_send, 0)

    @pl.when(at_edge)
    def _():
        def send_later(n, carry):
            send_parts(owner(n))
            return carry

        lax.fori_loop(0, NF, send_later, 0)

    pltpu.make_async_copy(depths.at[own], depth_rx.at[mine], depth_recv.at[mine]).start()
    for least, most, at, count in PARTS:
        @pl.when((mine >= least) & (mine <= most))
        def _():
            pltpu.make_async_copy(
                out.at[pl.ds(own * W + at, count)], rx.at[mine + 2, pl.ds(at, count)], recv.at[mine + 2]
            ).start()

    for b in range(NB):
        wait_bytes(depth_rx.at[b], depth_recv.at[b])
    for slot in range(2, NB + 2):
        first, last = max(slot - 4, 0), min(slot, NB - 1)
        wait_bytes(rx.at[slot, pl.ds(first - slot + 4, last - first + 1)], recv.at[slot])
    for slot, at, count, there in outer:
        @pl.when(there)
        def _():
            wait_bytes(rx.at[slot, pl.ds(at, count)], recv.at[slot])

    def settle(s, carry):
        i = (own + s) % NF
        to_sibling(i).wait_send()
        for b, at, count, slot, where, there in rims:
            @pl.when((mine == b) & there)
            def _():
                rim_copy(i, at, count, slot, where).wait_send()

        @pl.when(i != own)
        def _():
            depth_copy(i).wait_send()
            for least, most, at, count in PARTS:
                @pl.when((mine >= least) & (mine <= most))
                def _():
                    part_copy(i, at, count).wait_send()

        return carry

    lax.fori_loop(1, NF + 1, settle, 0)


def sum_kernel(depth_rx, rx, depth_out, grad_out):
    for b in range(NB):
        depth_out[:, b * 128:(b + 1) * 128] = depth_rx[b]
        total = rx[b, 4].astype(f32)
        for k in range(1, W):
            total += rx[b + k, 4 - k].astype(f32)
        grad_out[:, b * 128:(b + 1) * 128] = total


def per_device(features, views, offsets, kernels, reg_weight, head_weight, depth_cot):
    vmem = pl.BlockSpec(memory_space=pltpu.VMEM)
    smem = pl.BlockSpec(memory_space=pltpu.SMEM)
    hbm = pl.BlockSpec(memory_space=pltpu.HBM)
    dma = pltpu.SemaphoreType.DMA
    shape = jax.ShapeDtypeStruct

    win, index, cot, diag, band, columns = pl.pallas_call(
        exchange_kernel,
        name="exchange",
        out_shape=(
            shape((ZERO + 1, C, 128), bf16), shape((NF, 128), i32), shape((NF, 128), f32),
            shape((D // 2, 256, 256), bf16), shape((2 * D, D * C), bf16), shape((3, C, 128), f32),
        ),
        in_specs=[hbm] * 7,
        out_specs=(vmem,) * 6,
        scratch_shapes=[
            pltpu.VMEM((NB, C, 128), bf16),
            pltpu.VMEM((V, NB, D), i32),
            pltpu.VMEM((1, NB * 128), f32),
            pltpu.VMEM((3, 8, C), bf16),
            pltpu.SMEM((V, 16), i32),
            pltpu.SMEM((8,), f32),
            pltpu.VMEM((NB, 1, 256), f32),
            pltpu.VMEM((NF, 1, 256), f32),
            dma((NB,)), dma((NF,)), dma((NB,)), dma((NF,)), dma((4,)), dma((NF,)), dma((NF,)), dma((8,)),
        ],
        compiler_params=pltpu.CompilerParams(
            collective_id=0, has_side_effects=True, vmem_limit_bytes=16 << 20
        ),
    )(
        *(
            pltpu.with_memory_space_constraint(x, pltpu.HBM)
            for x in (
                features.reshape(C, NB * 128), jnp.transpose(offsets[0], (0, 2, 1)), depth_cot, views.T,
                kernels.reshape(D // 2, 2, 128, 128), reg_weight, head_weight,
            )
        )
    )

    depths, acc, ref_acc = pl.pallas_call(
        compute_kernel,
        name="compute",
        out_shape=(shape((NF, 1, 128), f32), shape((ZERO + 1, C, 128), f32), shape((NF, C, 128), f32)),
        in_specs=[smem] + [vmem] * 5,
        out_specs=(vmem,) * 3,
        scratch_shapes=[
            pltpu.VMEM((D, NF, V + 1, C, 128), bf16),
            pltpu.VMEM((D * C, NF * 128), bf16),
            pltpu.VMEM((NF, D, 128), f32),
        ],
        compiler_params=pltpu.CompilerParams(vmem_limit_bytes=40 << 20),
    )(index, win, diag, band, columns, cot)

    depth_rx, rx = pl.pallas_call(
        return_kernel,
        name="give_back",
        out_shape=(shape((NB, 1, 128), f32), shape((NB + 4, W, C, 128), bf16)),
        in_specs=[vmem] * 3,
        out_specs=(vmem,) * 2,
        scratch_shapes=[
            pltpu.VMEM((NF * W, C, 128), bf16),
            pltpu.VMEM((NF * W, C, 128), bf16),
            pltpu.VMEM((NF * W, C, 128), bf16),
            dma((NF,)), dma((NB + 4,)), dma((NF,)), dma((NF,)), dma((NB,)), dma((NF,)), dma((NF,)),
        ],
        compiler_params=pltpu.CompilerParams(
            collective_id=1, has_side_effects=True, vmem_limit_bytes=16 << 20
        ),
    )(acc, ref_acc, depths)

    depth_map, grad = pl.pallas_call(
        sum_kernel,
        name="total",
        out_shape=(shape((1, NB * 128), f32), shape((C, NB * 128), f32)),
        in_specs=[vmem] * 2,
        out_specs=(vmem,) * 2,
        compiler_params=pltpu.CompilerParams(vmem_limit_bytes=8 << 20),
    )(depth_rx, rx)
    return depth_map, grad.reshape(1, C, NB * 128)


def solution(mesh):
    return jax.shard_map(
        per_device,
        mesh=mesh,
        in_specs=(
            P("frame", None, "tile"),
            P(),
            P("frame", None, None, "tile"),
            P(),
            P(),
            P(),
            P("frame", "tile"),
        ),
        out_specs=(P("frame", "tile"), P("frame", None, "tile")),
        check_vma=False,
    )
```
